768 devices in a mesh: dp: 16 (over x, z_hi, core), fsdp: 48 (over y, z_lo).
Axes of the slice: x: 4, y: 8, z: 12 (z_hi: 2, z_lo: 6; z = z_hi * 6 + z_lo), core: 2. Of those that a mesh axis runs over, the one named last changes fastest.
Arguments:
- loader_rows: bfloat16 [16, 25344, 512], P('dp', 'fsdp'), may hold values from -6 to 6
- dest_list: int32 [16, 25344], P('dp', 'fsdp'), may hold values from 0 to 12287, as said below
- row_counts: int32 [16, 48], P('dp', 'fsdp'), may hold values from 0 to 528, as said below
- bucket_ids: int32 [16, 48], P('dp', 'fsdp'), may hold values from 0 to 2
- conv_weight: bfloat16 [4608, 256], P('fsdp'), may hold values from -0.09375 to 0.09375
- out_grad: bfloat16 [16, 12288, 256], P('dp', 'fsdp'), may hold values from -6 to 6
Outputs:
- section_out: bfloat16 [16, 12288, 256], P('dp', 'fsdp')
- input_grad: bfloat16 [16, 12288, 512], P('dp', 'fsdp')
- conv_grad: float32 [4608, 256], P('fsdp')
The draws below stay inside these ranges and needn't reach their ends.
Inputs may be any that keep to these rules, and one draw needn't show every extreme that they name: `dest_list`: in each data group the used slots of all loader devices name each of the group's 12288 feature rows exactly once. From one loader device to the 256 rows of one device go at most 11 used slots, and every device receives exactly 11 from some loader device. Entries past a loader's count are arbitrary values in range. `row_counts`: the counts of a data group sum to 12288; in each data group some loader device uses all 528 slots.
All inputs are finite; a program needn't handle non-finite values.
Results may differ from the reference program's by a relative error of at most 0.0031.
Values may be sent and summed in bfloat16 or wider, within the bound.
A program may use at most 64 MiB of HBM per device.

```python
import math
import jax
import jax.numpy as jnp
from jax import lax

CIN = 512
COUT = 256
GROUPS = 32
PIX = 256
IMG_DEV = 1
GROUP_ROWS = 12288
CAP = 11
LOAD = 528
TOTAL_ROWS = 196608
N_DP = 16
N_FSDP = 48


def route_tables(key):
    rows_dev = IMG_DEV * PIX
    peers = N_FSDP
    groups = N_DP
    key_rank, key_move, key_place, key_shuffle, key_junk = jax.random.split(key, 5)
    quota = rows_dev // peers
    leftover = rows_dev % peers
    ordered = jnp.arange(peers, dtype=jnp.int32)
    base_values = quota + (ordered < leftover).astype(jnp.int32)
    taker_values = base_values[0::2]
    giver_values = base_values[1::2]
    move_limit = jnp.minimum(giver_values, CAP - taker_values)
    ranking = jax.vmap(lambda sub_key: jax.random.permutation(sub_key, peers))(jax.random.split(key_rank, groups)).astype(jnp.int32)
    moved = jax.random.randint(key_move, (groups, peers, peers // 2), 0, move_limit + 1).astype(jnp.int32)
    moved = moved.at[:, :, 0].set(move_limit[0])
    ordered_amounts = jnp.stack([taker_values + moved, giver_values - moved], axis=-1).reshape(groups, peers, peers)
    picked = jnp.broadcast_to(ranking[:, None, :], ordered_amounts.shape)
    amounts = jnp.take_along_axis(ordered_amounts, picked, axis=2).transpose(0, 2, 1)
    offsets = jnp.cumsum(amounts, axis=1) - amounts
    counts = jnp.sum(amounts, axis=2).astype(jnp.int32)
    position_perm = jax.vmap(lambda sub_key: jax.random.permutation(sub_key, rows_dev))(jax.random.split(key_place, groups * peers)).reshape(groups, peers, rows_dev).astype(jnp.int32)
    within = jnp.arange(CAP, dtype=jnp.int32)
    usable = within[None, None, None, :] < amounts[..., None]
    lookup = jnp.minimum(offsets[..., None] + within, rows_dev - 1)
    group_index = jnp.arange(groups, dtype=jnp.int32)[:, None, None, None]
    peer_index = jnp.arange(peers, dtype=jnp.int32)[None, None, :, None]
    positions = position_perm[group_index, peer_index, lookup]
    destinations = (peer_index * rows_dev + positions).reshape(groups, peers, LOAD)
    usable_flat = usable.reshape(groups, peers, LOAD)
    shuffled = jax.vmap(lambda sub_key: jax.random.permutation(sub_key, LOAD))(jax.random.split(key_shuffle, groups * peers)).reshape(groups, peers, LOAD).astype(jnp.int32)
    scores = (1 - usable_flat.astype(jnp.int32)) * LOAD + shuffled
    ordering = jnp.argsort(scores, axis=-1, stable=True)
    sorted_dest = jnp.take_along_axis(destinations, ordering, axis=-1)
    sorted_usable = jnp.take_along_axis(usable_flat, ordering, axis=-1)
    junk_values = jax.random.randint(key_junk, (groups, peers, LOAD), 0, peers * rows_dev).astype(jnp.int32)
    final_dest = jnp.where(sorted_usable, sorted_dest, junk_values).astype(jnp.int32)
    return (final_dest.reshape(groups, peers * LOAD), counts)


def draw_dest_list(key, part):
    return route_tables(jax.random.fold_in(key, 7))[0]


def draw_row_counts(key, part):
    return route_tables(jax.random.fold_in(key, 7))[1]


def set_ends(drawn, own_key, low, top_value):
    extent = drawn.shape
    place = [jax.random.randint(jax.random.fold_in(own_key, axis), (), 0, extent[axis]) for axis in range(len(extent))]
    drawn = drawn.at[tuple(place)].set(low)
    longest = extent.index(max(extent))
    place[longest] = (place[longest] + 1) % extent[longest]
    return drawn.at[tuple(place)].set(top_value)


def levels(own_key, dims, cuts, low, top_value):
    level, own = 1.0, jax.random.fold_in(own_key, 6)
    for axis_at, shards_of in cuts:
        heights = jnp.exp(jax.random.uniform(jax.random.fold_in(own, axis_at), (shards_of,), jnp.float32, low / len(cuts), top_value / len(cuts)))
        level = level * jnp.repeat(heights, dims[axis_at] // shards_of).reshape([-1 if axis == axis_at else 1 for axis in range(len(dims))])
    return level


def gaussian(stream_key, extent, scale, most, cuts=(), held_as=jnp.bfloat16):
    values = scale * jax.random.normal(stream_key, extent, jnp.float32)
    if cuts:
        values = values * levels(stream_key, extent, cuts, -0.22, 0.18)
    return jnp.clip(values, -most, most).astype(held_as)


def setup_inputs(seed: int = 0) -> dict:
    seeds = jax.random.split(jax.random.key(seed), 7)
    return {
        "loader_rows": gaussian(seeds[0], (N_DP, N_FSDP * LOAD, CIN), 1.0, 6.0, ((0, 16), (1, 48))),
        "dest_list": draw_dest_list(jax.random.fold_in(seeds[6], 71), 0),
        "row_counts": draw_row_counts(jax.random.fold_in(seeds[6], 71), 0),
        "bucket_ids": set_ends(jax.random.randint(seeds[3], (N_DP, N_FSDP * IMG_DEV), 0, 3), jax.random.fold_in(seeds[3], 1), 0, 2).astype(jnp.int32),
        "conv_weight": gaussian(seeds[4], (9 * CIN, COUT), (9 * CIN) ** -0.5, 0.09375, ((0, 48),)),
        "out_grad": gaussian(seeds[5], (N_DP, GROUP_ROWS, COUT), 1.0, 6.0, ((0, 16), (1, 48))),
    }


def activate(values):
    pixels = values.shape[0]
    grouped = values.reshape(pixels, GROUPS, -1)
    centre = lax.optimization_barrier(jnp.mean(grouped, axis=(0, 2), keepdims=True))
    centred = grouped - centre
    spread = lax.optimization_barrier(jnp.mean(centred * centred, axis=(0, 2), keepdims=True))
    return jax.nn.silu(centred * lax.rsqrt(spread + 1e-05)).reshape(values.shape)

def neighbours(bucket, pixels):
    width = jnp.left_shift(jnp.int32(8), bucket.astype(jnp.int32))
    height = pixels // width
    places = jnp.arange(pixels, dtype=jnp.int32)
    row_of = places // width
    column_of = places % width
    sources = []
    inside = []
    for offset_y in (-1, 0, 1):
        for offset_x in (-1, 0, 1):
            near_row = row_of + offset_y
            near_column = column_of + offset_x
            within = (near_row >= 0) & (near_row < height) & (near_column >= 0) & (near_column < width)
            sources.append(jnp.where(within, near_row * width + near_column, 0).astype(jnp.int32))
            inside.append(within)
    return (sources, inside)

def unfold(hidden, sources, inside):
    taps = [jnp.where(inside[tap_index][:, None], hidden[sources[tap_index]], jnp.zeros((), hidden.dtype)) for tap_index in range(9)]
    return jnp.concatenate(taps, axis=1)

def fold_back(back, sources, inside, channels):
    gathered = jnp.zeros((back.shape[0], channels), jnp.float32)
    for tap_index in range(9):
        mirror = 8 - tap_index
        block_cols = back[:, tap_index * channels:(tap_index + 1) * channels]
        gathered = gathered + jnp.where(inside[mirror][:, None], block_cols[sources[mirror]], jnp.zeros((), jnp.float32))
    return gathered

def image_step(picture, bucket, weight, cotangent):
    channels = picture.shape[1]
    out_width = cotangent.shape[1]
    sources, inside = neighbours(bucket, picture.shape[0])
    widened = picture.astype(jnp.float32)
    activated, pullback = jax.vjp(activate, widened)
    hidden = activated.astype(jnp.bfloat16)
    columns = unfold(hidden, sources, inside)
    conv_part = jnp.dot(columns, weight, preferred_element_type=jnp.float32)
    section = (widened[:, :out_width] + conv_part).astype(jnp.bfloat16)
    back = lax.dot_general(cotangent, weight, (((1,), (1,)), ((), ())), preferred_element_type=jnp.float32)
    hidden_grad = fold_back(back, sources, inside, channels)
    widened_grad = pullback(hidden_grad)[0]
    widened_grad = widened_grad.at[:, :out_width].add(cotangent.astype(jnp.float32))
    return (section, widened_grad.astype(jnp.bfloat16), columns)

def reference(loader_rows, dest_list, row_counts, bucket_ids, conv_weight, out_grad):
    groups = dest_list.shape[0]
    spread_slots = dest_list.shape[1]
    slot_index = jnp.arange(spread_slots, dtype=jnp.int32) % LOAD
    usable = slot_index[None, :] < jnp.repeat(row_counts, LOAD, axis=1)
    target = jnp.where(usable, dest_list, GROUP_ROWS).astype(jnp.int32)
    group_index = jnp.arange(groups, dtype=jnp.int32)[:, None]
    placed = jnp.zeros((groups, GROUP_ROWS, CIN), jnp.bfloat16).at[group_index, target].set(loader_rows, mode='drop')
    images = placed.reshape(-1, PIX, CIN)
    cotangents = out_grad.reshape(-1, PIX, COUT)
    buckets = bucket_ids.reshape(-1)
    image_count = images.shape[0]
    block_size = math.gcd(image_count, 8)
    block_count = image_count // block_size
    stacked = (images.reshape(block_count, block_size, PIX, CIN), buckets.reshape(block_count, block_size), cotangents.reshape(block_count, block_size, PIX, COUT))

    def one_block(running, pieces):
        block_images, block_buckets, block_grads = pieces

        def single(picture, bucket, cotangent):
            return image_step(picture, bucket, conv_weight, cotangent)
        outputs, input_grads, columns = jax.vmap(single)(block_images, block_buckets, block_grads)
        weight_term = jnp.einsum('bpk,bpo->ko', columns.astype(jnp.float32), block_grads.astype(jnp.float32))
        return (running + weight_term, (outputs, input_grads))
    summed, (outputs, input_grads) = lax.scan(one_block, jnp.zeros((9 * CIN, COUT), jnp.float32), stacked)
    conv_grad = summed * (1.0 / math.sqrt(TOTAL_ROWS))
    section_out = outputs.reshape(groups, GROUP_ROWS, COUT)
    input_grad = input_grads.reshape(groups, GROUP_ROWS, CIN)
    return (section_out, input_grad, conv_grad)
```

```python
import functools

import jax
import jax.numpy as jnp
from jax import lax
from jax.experimental import pallas as pl
from jax.experimental.pallas import tpu as pltpu
from jax.sharding import PartitionSpec as P

GROUPS = 32
TAPS = 9
LANES = 128
MESH = pl.DeviceIdType.MESH
BF16 = jnp.bfloat16
F32 = jnp.float32
I32 = jnp.int32


def layout(mesh):
    dp, fsdp = mesh.shape["dp"], mesh.shape["fsdp"]
    across, height = (4, 2), 8
    if fsdp % height:
        height = 3
    if dp % 16:
        across = (4, 1)
    return across[0], across[1], height, fsdp // height


def dot(a, b, dims=((1,), (0,))):
    return lax.dot_general(a, b, (dims, ((), ())), preferred_element_type=F32)


def iota(shape, dim):
    return lax.broadcasted_iota(I32, shape, dim)


def group_total(row, size):
    width = row.shape[1]
    lane = iota(row.shape, 1)
    step = 1
    while step < size:
        up = pltpu.roll(row, width - step, 1)
        down = pltpu.roll(row, step, 1)
        row = row + jnp.where((lane & step) == 0, up, down)
        step *= 2
    return row


def column_sum(values):
    total = jnp.sum(values, axis=0, keepdims=True)
    return jnp.broadcast_to(total, (8, values.shape[1]))


def kernel(
    sizes,
    slots_ref, dest_ref, count_ref, bucket_ref, shard_ref, grad_ref,
    section_ref, igrad_ref, cgrad_ref,
    wide, send, recv, weight, shifts, gcols, xhat_ref, rstd_ref, hidden_ref, hidden_t, hgrad,
    wgrad, core_out, core_in, x_out, x_own, x_in, y_out, y_own, y_in, z_out, z_in, quarters,
    local_sem, a2a_s, a2a_r, wz_s, wz_r, wy_s, wy_r, wx_s, wx_r, wc_s, wc_r,
    gc_s, gc_r, gx_s, gx_r, gy_s, gy_r, gz_s, gz_r, gf_s, gf_r,
):
    X, H, Y, Z = sizes
    HZ = Z // 2
    peers = Y * Z
    load, channels = slots_ref.shape
    pixels, out_width = grad_ref.shape
    chunks = channels // LANES
    cap = load // peers
    block = (cap + 1) * chunks
    rows_w = weight.shape[2]
    dp = lax.axis_index("dp")
    me = lax.axis_index("fsdp")
    core = lax.rem(dp, 2)
    zh = lax.rem(lax.div(dp, 2), H)
    x = lax.div(dp, 2 * H)
    y = lax.div(me, Z)
    z = lax.rem(me, Z)
    active = lax.div(z, HZ) == core

    def dp_at(x_, zh_, core_):
        return (x_ * H + zh_) * 2 + core_

    def around(value, extent):
        return lax.rem(value + extent, extent)

    barrier = pltpu.get_barrier_semaphore()

    def greet(dp_, fsdp_):
        pl.semaphore_signal(barrier, inc=1, device_id=(dp_, fsdp_), device_id_type=MESH)

    def greet_plane(k, _):
        greet(dp, lax.rem(me + k, peers))
        return 0

    lax.fori_loop(1, peers, greet_plane, 0)
    for dx in range(1, X):
        for other in range(2):
            greet(dp_at(lax.rem(x + dx, X), zh, other), me)
    greet(dp_at(x, zh, 1 - core), me)
    for dh in range(1, H):
        for tz in range(Z):
            greet(dp_at(x, lax.rem(zh + dh, H), core), y * Z + tz)
    greeted = peers - 1 + 2 * (X - 1) + 1 + (H - 1) * Z

    dest = dest_ref[...]
    usable = iota(dest.shape, 1) < count_ref[...]
    owner = jnp.where(usable, lax.div(dest, pixels), -1)
    place = lax.rem(dest, pixels)
    owns = iota((peers, load), 0) == owner
    owns_f = jnp.where(owns, 1.0, 0.0)
    before = jnp.where(iota((load, load), 0) < iota((load, load), 1), 1.0, 0.0).astype(BF16)
    earlier = dot(owns_f.astype(BF16), before)
    rank = jnp.sum(owns_f * earlier, axis=0, keepdims=True).astype(I32)
    slot = jnp.where(usable, owner * (cap + 1) + rank, -1)
    rows_all = peers * (cap + 1)
    pick = jnp.where(iota((rows_all, load), 0) == slot, 1.0, 0.0).astype(BF16)
    packed = dot(pick, slots_ref[...])
    for c in range(chunks):
        wide[pl.ds(c, rows_all, stride=chunks), :] = packed[:, c * LANES : (c + 1) * LANES]
    marks = jnp.where(
        iota((LANES, load), 0) == rank, (place - pixels).astype(F32), 0.0
    ).astype(BF16)
    places = dot(owns_f.astype(BF16), marks, ((1,), (1,))) + float(pixels)
    wide[pl.ds(cap * chunks, peers, stride=block), :] = places
    send[...] = wide[...].astype(BF16).reshape(send.shape)

    pl.semaphore_wait(barrier, greeted)

    def remote(src, dst, s_sem, r_sem, where):
        return pltpu.make_async_remote_copy(
            src_ref=src, dst_ref=dst, send_sem=s_sem, recv_sem=r_sem, device_id=where, device_id_type=MESH
        )

    def lanes_of(x_):
        return pl.ds(pl.multiple_of(lax.rem(x_, 2) * LANES, LANES), LANES)

    def w_quarter(b, x_):
        return weight.at[b, lax.div(x_, 2), :, lanes_of(x_)]

    def w_chunk(y_, x_, core_):
        return weight.at[pl.ds(Z * y_ + HZ * core_, HZ), lax.div(x_, 2), :, lanes_of(x_)]

    shard_quarter = shard_ref.at[lax.div(x, 2), :, lanes_of(x)]

    def wz_copy(dz, target, b):
        return remote(shard_quarter, w_quarter(b, x), wz_s.at[dz], wz_r.at[dz], (dp, y * Z + target))

    def wy_copy(dy, y_src, y_dst):
        part = w_chunk(y_src, x, core)
        return remote(part, part, wy_s.at[dy], wy_r.at[dy], (dp, y_dst * Z + z))

    def wx_copy(dx, k, y_, x_src, x_dst):
        part = w_chunk(y_, x_src, core)
        return remote(part, part, wx_s.at[dx, k], wx_r.at[dx, k], (dp_at(x_dst, zh, core), me))

    def wc_copy(dx, k, y_, x_src, core_):
        part = w_chunk(y_, x_src, core_)
        return remote(part, part, wc_s.at[dx, k], wc_r.at[dx, k], (dp_at(x, zh, 1 - core), me))

    def a2a_copy(k, source, target):
        return remote(send.at[target], recv.at[source], a2a_s.at[k], a2a_r.at[k], (dp, target))

    def a2a_peer(k, sign):
        ty = around(y + sign * lax.div(k, Z), Y)
        tz = around(z + sign * lax.rem(k, Z), Z)
        return ty * Z + tz

    @pl.when(active)
    def _():
        own = pltpu.make_async_copy(shard_quarter, w_quarter(me, x), local_sem)
        own.start()
        for dz in range(1, Z):
            wz_copy(dz, around(z + dz, Z), me).start()
        own.wait()

    def a2a_start(k, _):
        a2a_copy(k, me, a2a_peer(k, 1)).start()
        return 0

    lax.fori_loop(1, peers, a2a_start, 0)
    recv[me] = send[me]

    bucket = bucket_ref[...]
    width = jnp.where(bucket == 0, 8, jnp.where(bucket == 1, 16, 32))
    grad = grad_ref[...]
    pixel = iota((pixels, pixels), 0)
    gap = iota((pixels, pixels), 1) - pixel
    column = pixel & (width - 1)

    def make_shift(t, _):
        a = lax.div(t, 3) - 1
        b = lax.rem(t, 3) - 1
        near = column + b
        hit = (gap == a * width + b) & (near >= 0) & (near < width)
        shift = jnp.where(hit, 1.0, 0.0).astype(BF16)
        shifts[t] = shift
        gcols[TAPS - 1 - t] = dot(shift, grad).astype(BF16)
        return 0

    lax.fori_loop(0, TAPS, make_shift, 0)

    for j in range(HZ):
        sz = HZ * core + j

        @pl.when(sz != z)
        def _(sz=sz):
            wz_copy(around(z - sz, Z), z, y * Z + sz).wait_recv()

    for dy in range(1, Y):
        wy_copy(dy, y, lax.rem(y + dy, Y)).start()

    def w_forward(k, _):
        sy = around(y - k, Y)

        @pl.when(k > 0)
        def _():
            wy_copy(k, sy, y).wait_recv()

        for dx in range(1, X):
            wx_copy(dx, k, sy, x, lax.rem(x + dx, X)).start()
        wc_copy(0, k, sy, x, core).start()
        return 0

    lax.fori_loop(0, Y, w_forward, 0)

    def w_cross(k, _):
        sy = around(y - k, Y)
        for dx in range(1, X):
            sx = around(x - dx, X)
            wx_copy(dx, k, sy, sx, x).wait_recv()
            wc_copy(dx, k, sy, sx, core).start()
        return 0

    lax.fori_loop(0, Y, w_cross, 0)

    def a2a_wait(k, _):
        a2a_copy(k, a2a_peer(k, -1), me).wait_recv()
        return 0

    lax.fori_loop(1, peers, a2a_wait, 0)
    wide[...] = recv[...].astype(F32).reshape(wide.shape)
    got_places = wide[pl.ds(cap * chunks, peers, stride=block), :].astype(BF16)
    index = iota((peers, rows_all), 1)
    spread = jnp.where(lax.div(index, cap + 1) == iota((peers, rows_all), 0), 1.0, 0.0).astype(BF16)
    by_rank = dot(got_places, spread, ((0,), (0,)))
    index = iota((LANES, rows_all), 1)
    fits = lax.rem(index, cap + 1) == iota((LANES, rows_all), 0)
    where_to = jnp.sum(jnp.where(fits, by_rank, 0.0), axis=0, keepdims=True).astype(I32)
    put = jnp.where(iota((pixels, rows_all), 0) == where_to, 1.0, 0.0).astype(BF16)
    features = jnp.concatenate(
        [dot(put, wide[pl.ds(c, rows_all, stride=chunks), :].astype(BF16)) for c in range(chunks)], axis=1
    )
    per_group = channels // GROUPS
    share = 1.0 / float(pixels * per_group)
    centre = group_total(column_sum(features), per_group) * share
    centred = features - centre[:1]
    spread_of = group_total(column_sum(centred * centred), per_group) * share
    rstd = lax.rsqrt(spread_of + 1e-05)
    xhat = centred * rstd[:1]
    hidden = xhat * jax.nn.sigmoid(xhat)
    rstd_ref[...] = rstd
    xhat_ref[...] = xhat
    hidden_t[...] = hidden.T.astype(BF16)
    hidden_ref[...] = hidden.astype(BF16)
    section_ref[...] = features[:, :out_width]

    def w_term(t, _):
        wgrad[pl.ds(pl.multiple_of(t * channels, channels), channels), :] = dot(hidden_t[...], gcols[t])
        return 0

    lax.fori_loop(0, TAPS, w_term, 0)

    rows_b = 2 * rows_w
    span = HZ * rows_b

    def my_rows(y_, core_):
        return pl.ds(pl.multiple_of((Z * y_ + HZ * core_) * rows_b, rows_b), span)

    def gc_copy(k, y_):
        return remote(core_out.at[y_], core_in.at[y_], gc_s.at[k], gc_r.at[k], (dp_at(x, zh, 1 - core), me))

    def gx_copy(dx, k, y_, x_):
        return remote(x_out.at[x_, y_], x_in.at[dx, y_], gx_s.at[dx, k], gx_r.at[dx, k], (dp_at(x_, zh, core), me))

    def gy_copy(k, y_):
        return remote(y_out.at[k], y_in.at[k], gy_s.at[k], gy_r.at[k], (dp, y_ * Z + z))

    def core_stage(k, _):
        y_ = lax.rem(y + k, Y)
        core_out[y_] = wgrad[my_rows(y_, 1 - core), :].astype(BF16).reshape(core_out.shape[1:])
        gc_copy(k, y_).start()
        return 0

    lax.fori_loop(0, Y, core_stage, 0)

    def x_stage(k, _):
        y_ = lax.rem(y + k, Y)
        gc_copy(k, y_).wait_recv()
        both = wgrad[my_rows(y_, core), :].reshape(core_in.shape[1:]) + core_in[y_].astype(F32)
        own = None
        for x_ in range(X):
            first = (x_ % 2) * LANES
            part = both[:, x_ // 2, :, first : first + LANES]
            x_out[x_, y_] = part.astype(BF16)
            own = part if own is None else jnp.where(x == x_, part, own)
        x_own[y_] = own
        for dx in range(1, X):
            gx_copy(dx, k, y_, lax.rem(x + dx, X)).start()
        return 0

    lax.fori_loop(0, Y, x_stage, 0)

    def w_last(k, _):
        sy = around(y - k, Y)
        for dx in range(X):
            wc_copy(dx, k, sy, around(x - dx, X), 1 - core).wait_recv()
        return 0

    lax.fori_loop(0, Y, w_last, 0)
    hgrad[...] = jnp.zeros_like(hgrad)
    taps_row = 3
    blocks_row = taps_row * channels // (2 * rows_w)

    def conv_row(i, _):
        kernel_row = weight[pl.ds(i * blocks_row, blocks_row)].reshape(taps_row * channels, out_width)
        for j in range(taps_row):
            t = i * taps_row + j
            tap = kernel_row[j * channels : (j + 1) * channels]
            hgrad[...] += dot(gcols[t], tap, ((1,), (1,)))
            near = dot(shifts[t], hidden_ref[...]).astype(BF16)
            section_ref[...] += dot(near, tap)
        return 0

    lax.fori_loop(0, TAPS // taps_row, conv_row, 0)
    xhat = xhat_ref[...]
    gate = jax.nn.sigmoid(xhat)
    slope = hgrad[...] * (gate * (1.0 + xhat * (1.0 - gate)))
    mean_s = group_total(column_sum(slope), per_group) * share
    mean_sx = group_total(column_sum(slope * xhat), per_group) * share
    back = rstd_ref[:1, :] * (slope - mean_s[:1] - xhat * mean_sx[:1])
    igrad_ref[:, :out_width] = (back[:, :out_width] + grad_ref[...].astype(F32)).astype(BF16)
    igrad_ref[:, out_width:] = back[:, out_width:].astype(BF16)

    def y_stage(k, _):
        y_ = lax.rem(y + k, Y)
        total = x_own[y_]
        for dx in range(1, X):
            gx_copy(dx, k, y_, x).wait_recv()
            total = total + x_in[dx, y_].astype(F32)

        y_own[...] = total
        y_out[k] = total.astype(BF16)
        gy_copy(k, y_).start()
        return 0

    lax.fori_loop(1, Y, y_stage, 0)
    total = x_own[y]
    for dx in range(1, X):
        gx_copy(dx, 0, y, x).wait_recv()
        total = total + x_in[dx, y].astype(F32)
    y_own[...] = total

    def y_add(k, _):
        gy_copy(k, y).wait_recv()
        y_own[...] += y_in[k].astype(F32)
        return 0

    lax.fori_loop(1, Y, y_add, 0)
    z_out[...] = y_own[...]

    def gz_copy(j, h_, sh, sz):
        return remote(z_out.at[j], z_in.at[sh, sz], gz_s.at[j, h_], gz_r.at[sh, sz], (dp_at(x, h_, core), y * Z + HZ * core + j))

    for j in range(HZ):
        for h_ in range(H):
            mine = (HZ * core + j == z) & (zh == h_)

            @pl.when(mine)
            def _(j=j):
                z_in[zh, z] = z_out[j]

            @pl.when(jnp.logical_not(mine))
            def _(j=j, h_=h_):
                gz_copy(j, h_, zh, z).start()

    def gf_copy(dx, core_, x_src, x_dst):
        return remote(quarters.at[x_src], quarters.at[x_src], gf_s.at[dx, core_], gf_r.at[x_src], (dp_at(x_dst, zh, core_), me))

    images = peers * dp_count(sizes)
    scale = 1.0 / float(images * pixels) ** 0.5

    @pl.when(active)
    def _():
        for h_ in range(H):
            for sz in range(Z):

                @pl.when(jnp.logical_not((zh == h_) & (z == sz)))
                def _(h_=h_, sz=sz):
                    gz_copy(0, 0, h_, sz).wait_recv()

        total = z_in[0, 0]
        for h_ in range(H):
            for sz in range(Z):
                if h_ or sz:
                    total = total + z_in[h_, sz]
        quarters[x] = total * scale
        gf_copy(0, 1 - core, x, x).start()
        for dx in range(1, X):
            for other in range(2):
                gf_copy(dx, other, x, lax.rem(x + dx, X)).start()

    for x_ in range(X):

        @pl.when(jnp.logical_not(active & (x == x_)))
        def _(x_=x_):
            gf_copy(0, 0, x_, x).wait_recv()

    for x_ in range(X):
        first = (x_ % 2) * LANES
        cgrad_ref[x_ // 2, :, first : first + LANES] = quarters[x_]

    def a2a_left(k, _):
        a2a_copy(k, me, a2a_peer(k, 1)).wait_send()
        return 0

    lax.fori_loop(1, peers, a2a_left, 0)

    @pl.when(active)
    def _():
        for dz in range(1, Z):
            wz_copy(dz, around(z + dz, Z), me).wait_send()
        gf_copy(0, 1 - core, x, x).wait_send()
        for dx in range(1, X):
            for other in range(2):
                gf_copy(dx, other, x, lax.rem(x + dx, X)).wait_send()

    for j in range(HZ):
        for h_ in range(H):

            @pl.when(jnp.logical_not((HZ * core + j == z) & (zh == h_)))
            def _(j=j, h_=h_):
                gz_copy(j, h_, zh, z).wait_send()

    for dy in range(1, Y):
        wy_copy(dy, y, lax.rem(y + dy, Y)).wait_send()
        gy_copy(dy, lax.rem(y + dy, Y)).wait_send()

    def rest_left(k, _):
        y_ = lax.rem(y + k, Y)
        sy = around(y - k, Y)
        gc_copy(k, y_).wait_send()
        wc_copy(0, k, sy, x, core).wait_send()
        for dx in range(1, X):
            wc_copy(dx, k, sy, around(x - dx, X), core).wait_send()
            wx_copy(dx, k, sy, x, lax.rem(x + dx, X)).wait_send()
            gx_copy(dx, k, y_, lax.rem(x + dx, X)).wait_send()
        return 0

    lax.fori_loop(0, Y, rest_left, 0)


def dp_count(sizes):
    return sizes[0] * sizes[1] * 2


def on_device(sizes, loader_rows, dest_list, row_counts, bucket_ids, conv_weight, out_grad):
    X, H, Y, Z = sizes
    HZ = Z // 2
    peers = Y * Z
    load, channels = loader_rows.shape[1:]
    pixels, out_width = out_grad.shape[1:]
    chunks = channels // LANES
    block = (load // peers + 1) * chunks
    rows_w = conv_weight.shape[0] // 2
    vmem = pltpu.VMEM
    sem = pltpu.SemaphoreType.DMA
    part = (HZ, rows_w, LANES)
    scratch = [
        vmem((peers * block, LANES), F32),
        vmem((peers, block, LANES), BF16),
        vmem((peers, block, LANES), BF16),
        vmem((peers, 2, rows_w, out_width), BF16),
        vmem((TAPS, pixels, pixels), BF16),
        vmem((TAPS, pixels, out_width), BF16),
        vmem((pixels, channels), F32),
        vmem((8, channels), F32),
        vmem((pixels, channels), BF16),
        vmem((channels, pixels), BF16),
        vmem((pixels, channels), F32),
        vmem((TAPS * channels, out_width), F32),
        vmem((Y, HZ, 2, rows_w, out_width), BF16),
        vmem((Y, HZ, 2, rows_w, out_width), BF16),
        vmem((X, Y, *part), BF16),
        vmem((Y, *part), F32),
        vmem((X, Y, *part), BF16),
        vmem((Y, *part), BF16),
        vmem(part, F32),
        vmem((Y, *part), BF16),
        vmem(part, F32),
        vmem((H, Z, rows_w, LANES), F32),
        vmem((X, rows_w, LANES), F32),
        sem,
        sem((peers,)), sem((peers,)),
        sem((Z,)), sem((Z,)),
        sem((Y,)), sem((Y,)),
        sem((X, Y)), sem((X, Y)),
        sem((X, Y)), sem((X, Y)),
        sem((Y,)), sem((Y,)),
        sem((X, Y)), sem((X, Y)),
        sem((Y,)), sem((Y,)),
        sem((HZ, H)), sem((H, Z)),
        sem((X, 2)), sem((X,)),
    ]
    whole = pl.BlockSpec(memory_space=pltpu.VMEM)
    flops = 2 * pixels * out_width * channels * TAPS * 3
    section, igrad, cgrad = pl.pallas_call(
        functools.partial(kernel, sizes),
        out_shape=(
            jax.ShapeDtypeStruct((pixels, out_width), F32),
            jax.ShapeDtypeStruct((pixels, channels), BF16),
            jax.ShapeDtypeStruct((2, rows_w, out_width), F32),
        ),
        in_specs=[whole] * 6,
        out_specs=(whole,) * 3,
        scratch_shapes=scratch,
        compiler_params=pltpu.CompilerParams(
            collective_id=0, has_side_effects=True, vmem_limit_bytes=48 * 2**20
        ),
        cost_estimate=pl.CostEstimate(flops=flops, bytes_accessed=2**21, transcendentals=0),
        name="residual_section",
    )(
        loader_rows[0],
        dest_list,
        row_counts,
        bucket_ids,
        conv_weight.reshape(2, rows_w, out_width),
        out_grad[0],
    )
    return section.astype(BF16)[None], igrad[None], cgrad.reshape(conv_weight.shape)


def solution(mesh):
    sizes = layout(mesh)
    in_specs = (
        P("dp", "fsdp", None),
        P("dp", "fsdp"),
        P("dp", "fsdp"),
        P("dp", "fsdp"),
        P("fsdp", None),
        P("dp", "fsdp", None),
    )
    out_specs = (P("dp", "fsdp", None), P("dp", "fsdp", None), P("fsdp", None))
    return jax.shard_map(
        functools.partial(on_device, sizes), mesh=mesh, in_specs=in_specs, out_specs=out_specs, check_vma=False
    )
```

```python
import functools

import jax
import jax.numpy as jnp
from jax import lax
from jax.experimental import pallas as pl
from jax.experimental.pallas import tpu as pltpu
from jax.sharding import PartitionSpec as P

GROUPS = 32
TAPS = 9
LANES = 128
MESH = pl.DeviceIdType.MESH
BF16 = jnp.bfloat16
F32 = jnp.float32
I32 = jnp.int32


def layout(mesh):
    dp, fsdp = mesh.shape["dp"], mesh.shape["fsdp"]
    across, height = (4, 2), 8
    if fsdp % height:
        height = 3
    if dp % 16:
        across = (4, 1)
    return across[0], across[1], height, fsdp // height


def dot(a, b, dims=((1,), (0,))):
    return lax.dot_general(a, b, (dims, ((), ())), preferred_element_type=F32)


def iota(shape, dim):
    return lax.broadcasted_iota(I32, shape, dim)


def group_total(row, size):
    width = row.shape[1]
    lane = iota(row.shape, 1)
    step = 1
    while step < size:
        up = pltpu.roll(row, width - step, 1)
        down = pltpu.roll(row, step, 1)
        row = row + jnp.where((lane & step) == 0, up, down)
        step *= 2
    return row


def column_sum(values):
    total = jnp.sum(values, axis=0, keepdims=True)
    return jnp.broadcast_to(total, (8, values.shape[1]))


def kernel(
    sizes,
    slots_hbm, dest_hbm, count_hbm, bucket_hbm, shard_ref, grad_hbm,
    section_hbm, igrad_hbm, cgrad_hbm,
    slots_ref, dest_ref, count_ref, bucket_ref, grad_ref, section_ref, section_out, igrad_ref, cgrad_ref,
    wide, send, recv, weight, shifts, gcols, xhat_ref, rstd_ref, hidden_ref, hidden_t, hgrad,
    wgrad, core_out, core_in, x_out, x_own, x_in, y_out, y_own, y_in, z_out, z_in, quarters,
    in_sem, out_sem, local_sem, a2a_s, a2a_r, wz_s, wz_r, wy_s, wy_r, wx_s, wx_r, wc_s, wc_r,
    gc_s, gc_r, gx_s, gx_r, gy_s, gy_r, gz_s, gz_r, gf_s, gf_r,
):
    X, H, Y, Z = sizes
    HZ = Z // 2
    peers = Y * Z
    load, channels = slots_ref.shape
    pixels, out_width = grad_ref.shape
    chunks = channels // LANES
    cap = load // peers
    block = (cap + 1) * chunks
    rows_w = weight.shape[2]
    dp = lax.axis_index("dp")
    me = lax.axis_index("fsdp")
    core = lax.rem(dp, 2)
    zh = lax.rem(lax.div(dp, 2), H)
    x = lax.div(dp, 2 * H)
    y = lax.div(me, Z)
    z = lax.rem(me, Z)
    active = lax.div(z, HZ) == core

    def dp_at(x_, zh_, core_):
        return (x_ * H + zh_) * 2 + core_

    def around(value, extent):
        return lax.rem(value + extent, extent)

    arriving = [
        pltpu.make_async_copy(src, dst, in_sem.at[n])
        for n, (src, dst) in enumerate(
            (
                (dest_hbm, dest_ref),
                (count_hbm, count_ref),
                (slots_hbm, slots_ref),
                (bucket_hbm, bucket_ref),
                (grad_hbm, grad_ref),
            )
        )
    ]
    for copy in arriving:
        copy.start()
    lanes = pl.ds(pl.multiple_of(lax.rem(x, 2) * LANES, LANES), LANES)
    own_piece = pltpu.make_async_copy(shard_ref.at[lax.div(x, 2), :, lanes], weight.at[x, me], local_sem)

    @pl.when(active)
    def _():
        own_piece.start()

    barrier = pltpu.get_barrier_semaphore()

    def greet(dp_, fsdp_):
        pl.semaphore_signal(barrier, inc=1, device_id=(dp_, fsdp_), device_id_type=MESH)

    def greet_plane(k, _):
        greet(dp, lax.rem(me + k, peers))
        return 0

    lax.fori_loop(1, peers, greet_plane, 0)
    for dx in range(1, X):
        for other in range(2):
            greet(dp_at(lax.rem(x + dx, X), zh, other), me)
    greet(dp_at(x, zh, 1 - core), me)
    for dh in range(1, H):
        for tz in range(Z):
            greet(dp_at(x, lax.rem(zh + dh, H), core), y * Z + tz)
    greeted = peers - 1 + 2 * (X - 1) + 1 + (H - 1) * Z

    for copy in arriving:
        copy.wait()
    dest = dest_ref[...]
    usable = iota(dest.shape, 1) < count_ref[...]
    owner = jnp.where(usable, lax.div(dest, pixels), -1)
    place = lax.rem(dest, pixels)
    owns = iota((peers, load), 0) == owner
    owns_f = jnp.where(owns, 1.0, 0.0)
    before = jnp.where(iota((load, load), 0) < iota((load, load), 1), 1.0, 0.0).astype(BF16)
    earlier = dot(owns_f.astype(BF16), before)
    rank = jnp.sum(owns_f * earlier, axis=0, keepdims=True).astype(I32)
    slot = jnp.where(usable, owner * (cap + 1) + rank, -1)
    rows_all = peers * (cap + 1)
    pick = jnp.where(iota((rows_all, load), 0) == slot, 1.0, 0.0).astype(BF16)
    packed = dot(pick, slots_ref[...])
    for c in range(chunks):
        wide[pl.ds(c, rows_all, stride=chunks), :] = packed[:, c * LANES : (c + 1) * LANES]
    marks = jnp.where(
        iota((LANES, load), 0) == rank, (place - pixels).astype(F32), 0.0
    ).astype(BF16)
    places = dot(owns_f.astype(BF16), marks, ((1,), (1,))) + float(pixels)
    wide[pl.ds(cap * chunks, peers, stride=block), :] = places
    send[...] = wide[...].astype(BF16).reshape(send.shape)

    pl.semaphore_wait(barrier, greeted)

    def remote(src, dst, s_sem, r_sem, where):
        return pltpu.make_async_remote_copy(
            src_ref=src, dst_ref=dst, send_sem=s_sem, recv_sem=r_sem, device_id=where, device_id_type=MESH
        )

    def w_quarter(b, x_):
        return weight.at[x_, b]

    def w_chunk(y_, x_, core_):
        return weight.at[x_, pl.ds(Z * y_ + HZ * core_, HZ)]

    def wz_copy(dz, target, b):
        part = w_quarter(b, x)
        return remote(part, part, wz_s.at[dz], wz_r.at[dz], (dp, y * Z + target))

    def wy_copy(k, y_src, y_dst):
        part = w_chunk(y_src, x, core)
        return remote(part, part, wy_s.at[k], wy_r.at[k], (dp, y_dst * Z + z))

    def wx_copy(dx, k, y_, x_src, x_dst):
        part = w_chunk(y_, x_src, core)
        return remote(part, part, wx_s.at[dx, k], wx_r.at[dx, k], (dp_at(x_dst, zh, core), me))

    def wc_copy(dx, k, y_, x_src, core_):
        part = w_chunk(y_, x_src, core_)
        return remote(part, part, wc_s.at[dx, k], wc_r.at[dx, k], (dp_at(x, zh, 1 - core), me))

    def a2a_copy(k, source, target):
        return remote(send.at[target], recv.at[source], a2a_s.at[k], a2a_r.at[k], (dp, target))

    def a2a_peer(k, sign):
        ty = around(y + sign * lax.div(k, Z), Y)
        tz = around(z + sign * lax.rem(k, Z), Z)
        return ty * Z + tz

    @pl.when(active)
    def _():
        own_piece.wait()
        for dz in range(1, Z):
            wz_copy(dz, around(z + dz, Z), me).start()

    def a2a_start(k, _):
        a2a_copy(k, me, a2a_peer(k, 1)).start()
        return 0

    lax.fori_loop(1, peers, a2a_start, 0)
    recv[me] = send[me]

    bucket = bucket_ref[...]
    width = jnp.where(bucket == 0, 8, jnp.where(bucket == 1, 16, 32))
    grad = grad_ref[...]
    pixel = iota((pixels, pixels), 0)
    gap = iota((pixels, pixels), 1) - pixel
    column = pixel & (width - 1)

    def make_shift(t, _):
        a = lax.div(t, 3) - 1
        b = lax.rem(t, 3) - 1
        near = column + b
        hit = (gap == a * width + b) & (near >= 0) & (near < width)
        shift = jnp.where(hit, 1.0, 0.0).astype(BF16)
        shifts[t] = shift
        gcols[TAPS - 1 - t] = dot(shift, grad).astype(BF16)
        return 0

    lax.fori_loop(0, TAPS, make_shift, 0, unroll=3)

    for j in range(HZ):
        sz = HZ * core + j

        @pl.when(sz != z)
        def _(sz=sz):
            wz_copy(around(z - sz, Z), z, y * Z + sz).wait_recv()

    for dy in range(1, Y):
        wy_copy(dy, y, lax.rem(y + dy, Y)).start()

    def w_forward(k, _):
        sy = around(y - k, Y)

        @pl.when(k > 0)
        def _():
            wy_copy(k, sy, y).wait_recv()

        for dx in range(1, X):
            wx_copy(dx, k, sy, x, lax.rem(x + dx, X)).start()
        wc_copy(0, k, sy, x, core).start()
        return 0

    lax.fori_loop(0, Y, w_forward, 0)

    def a2a_wait(k, _):
        a2a_copy(k, a2a_peer(k, -1), me).wait_recv()
        return 0

    lax.fori_loop(1, peers, a2a_wait, 0)
    wide[...] = recv[...].astype(F32).reshape(wide.shape)
    got_places = wide[pl.ds(cap * chunks, peers, stride=block), :].astype(BF16)
    index = iota((peers, rows_all), 1)
    spread = jnp.where(lax.div(index, cap + 1) == iota((peers, rows_all), 0), 1.0, 0.0).astype(BF16)
    by_rank = dot(got_places, spread, ((0,), (0,)))
    index = iota((LANES, rows_all), 1)
    fits = lax.rem(index, cap + 1) == iota((LANES, rows_all), 0)
    where_to = jnp.sum(jnp.where(fits, by_rank, 0.0), axis=0, keepdims=True).astype(I32)
    put = jnp.where(iota((pixels, rows_all), 0) == where_to, 1.0, 0.0).astype(BF16)
    features = jnp.concatenate(
        [dot(put, wide[pl.ds(c, rows_all, stride=chunks), :].astype(BF16)) for c in range(chunks)], axis=1
    )
    per_group = channels // GROUPS
    share = 1.0 / float(pixels * per_group)
    centre = group_total(column_sum(features), per_group) * share
    centred = features - centre[:1]
    spread_of = group_total(column_sum(centred * centred), per_group) * share
    rstd = lax.rsqrt(spread_of + 1e-05)
    xhat = centred * rstd[:1]
    hidden = xhat * jax.nn.sigmoid(xhat)
    rstd_ref[...] = rstd
    xhat_ref[...] = xhat
    hidden_t[...] = hidden.T.astype(BF16)
    hidden_ref[...] = hidden.astype(BF16)
    section_ref[...] = features[:, :out_width]

    def w_term(t, _):
        wgrad[pl.ds(pl.multiple_of(t * channels, channels), channels), :] = dot(hidden_t[...], gcols[t])
        return 0

    lax.fori_loop(0, TAPS, w_term, 0, unroll=True)

    rows_b = 2 * rows_w
    span = HZ * rows_b

    def my_rows(y_, core_):
        return pl.ds(pl.multiple_of((Z * y_ + HZ * core_) * rows_b, rows_b), span)

    def gc_copy(k, y_):
        return remote(core_out.at[y_], core_in.at[y_], gc_s.at[k], gc_r.at[k], (dp_at(x, zh, 1 - core), me))

    def gx_copy(dx, k, y_, x_):
        return remote(x_out.at[x_, y_], x_in.at[dx, y_], gx_s.at[dx, k], gx_r.at[dx, k], (dp_at(x_, zh, core), me))

    def gy_copy(k, y_):
        return remote(y_out.at[k], y_in.at[k], gy_s.at[k], gy_r.at[k], (dp, y_ * Z + z))

    def core_stage(k, _):
        y_ = lax.rem(y + k, Y)
        core_out[y_] = wgrad[my_rows(y_, 1 - core), :].astype(BF16).reshape(core_out.shape[1:])
        gc_copy(k, y_).start()
        return 0

    lax.fori_loop(0, Y, core_stage, 0)

    def x_stage(k, _):
        y_ = lax.rem(y + k, Y)
        gc_copy(k, y_).wait_recv()
        both = wgrad[my_rows(y_, core), :].reshape(core_in.shape[1:]) + core_in[y_].astype(F32)
        own = None
        for x_ in range(X):
            first = (x_ % 2) * LANES
            part = both[:, x_ // 2, :, first : first + LANES]
            x_out[x_, y_] = part.astype(BF16)
            own = part if own is None else jnp.where(x == x_, part, own)
        x_own[y_] = own
        for dx in range(1, X):
            gx_copy(dx, k, y_, lax.rem(x + dx, X)).start()
        return 0

    lax.fori_loop(0, Y, x_stage, 0)

    def w_cross(k, _):
        sy = around(y - k, Y)
        for dx in range(1, X):
            sx = around(x - dx, X)
            wx_copy(dx, k, sy, sx, x).wait_recv()
            wc_copy(dx, k, sy, sx, core).start()
        return 0

    lax.fori_loop(0, Y, w_cross, 0)

    def x_total(k, y_):
        total = x_own[y_]
        for dx in range(1, X):
            gx_copy(dx, k, y_, x).wait_recv()
            total = total + x_in[dx, y_].astype(F32)
        return total

    def y_stage(k, _):
        y_ = lax.rem(y + k, Y)
        y_out[k] = x_total(k, y_).astype(BF16)
        gy_copy(k, y_).start()
        return 0

    lax.fori_loop(1, Y, y_stage, 0)
    y_own[...] = x_total(0, y)

    def w_last(k, _):
        sy = around(y - k, Y)
        for dx in range(X):
            wc_copy(dx, k, sy, around(x - dx, X), 1 - core).wait_recv()
        return 0

    lax.fori_loop(0, Y, w_last, 0)
    hgrad[...] = jnp.zeros_like(hgrad)
    taps_row = 3
    blocks_row = taps_row * channels // (2 * rows_w)

    def conv_row(i, _):
        blocks = pl.ds(i * blocks_row, blocks_row)
        halves = [
            jnp.stack([weight[2 * r + h, blocks] for r in range(2)], axis=1).reshape(taps_row * channels, LANES)
            for h in range(2)
        ]
        kernel_row = jnp.concatenate(halves, axis=1)
        for j in range(taps_row):
            t = i * taps_row + j
            tap = kernel_row[j * channels : (j + 1) * channels]
            hgrad[...] += dot(gcols[t], tap, ((1,), (1,)))
            near = dot(shifts[t], hidden_ref[...]).astype(BF16)
            section_ref[...] += dot(near, tap)
        return 0

    lax.fori_loop(0, TAPS // taps_row, conv_row, 0)
    section_out[...] = section_ref[...].astype(BF16)
    xhat = xhat_ref[...]
    gate = jax.nn.sigmoid(xhat)
    slope = hgrad[...] * (gate * (1.0 + xhat * (1.0 - gate)))
    mean_s = group_total(column_sum(slope), per_group) * share
    mean_sx = group_total(column_sum(slope * xhat), per_group) * share
    back = rstd_ref[:1, :] * (slope - mean_s[:1] - xhat * mean_sx[:1])
    igrad_ref[:, :out_width] = (back[:, :out_width] + grad_ref[...].astype(F32)).astype(BF16)
    igrad_ref[:, out_width:] = back[:, out_width:].astype(BF16)
    leaving = [
        pltpu.make_async_copy(src, dst, out_sem.at[n])
        for n, (src, dst) in enumerate(
            ((section_out, section_hbm), (igrad_ref, igrad_hbm), (cgrad_ref, cgrad_hbm))
        )
    ]
    leaving[0].start()
    leaving[1].start()

    def y_add(k, _):
        gy_copy(k, y).wait_recv()
        y_own[...] += y_in[k].astype(F32)
        return 0

    lax.fori_loop(1, Y, y_add, 0)
    z_out[...] = y_own[...]

    def gz_copy(j, h_, sh, sz):
        return remote(z_out.at[j], z_in.at[sh, sz], gz_s.at[j, h_], gz_r.at[sh, sz], (dp_at(x, h_, core), y * Z + HZ * core + j))

    for j in range(HZ):
        for h_ in range(H):
            mine = (HZ * core + j == z) & (zh == h_)

            @pl.when(mine)
            def _(j=j):
                z_in[zh, z] = z_out[j]

            @pl.when(jnp.logical_not(mine))
            def _(j=j, h_=h_):
                gz_copy(j, h_, zh, z).start()

    def gf_copy(dx, core_, x_src, x_dst):
        return remote(quarters.at[x_src], quarters.at[x_src], gf_s.at[dx, core_], gf_r.at[x_src], (dp_at(x_dst, zh, core_), me))

    images = peers * dp_count(sizes)
    scale = 1.0 / float(images * pixels) ** 0.5

    @pl.when(active)
    def _():
        for h_ in range(H):
            for sz in range(Z):

                @pl.when(jnp.logical_not((zh == h_) & (z == sz)))
                def _(h_=h_, sz=sz):
                    gz_copy(0, 0, h_, sz).wait_recv()

        total = z_in[0, 0]
        for h_ in range(H):
            for sz in range(Z):
                if h_ or sz:
                    total = total + z_in[h_, sz]
        quarters[x] = total * scale
        gf_copy(0, 1 - core, x, x).start()
        for dx in range(1, X):
            for other in range(2):
                gf_copy(dx, other, x, lax.rem(x + dx, X)).start()

    for x_ in range(X):

        @pl.when(jnp.logical_not(active & (x == x_)))
        def _(x_=x_):
            gf_copy(0, 0, x_, x).wait_recv()

    for x_ in range(X):
        first = (x_ % 2) * LANES
        cgrad_ref[x_ // 2, :, first : first + LANES] = quarters[x_]
    leaving[2].start()

    def a2a_left(k, _):
        a2a_copy(k, me, a2a_peer(k, 1)).wait_send()
        return 0

    lax.fori_loop(1, peers, a2a_left, 0)

    @pl.when(active)
    def _():
        for dz in range(1, Z):
            wz_copy(dz, around(z + dz, Z), me).wait_send()
        gf_copy(0, 1 - core, x, x).wait_send()
        for dx in range(1, X):
            for other in range(2):
                gf_copy(dx, other, x, lax.rem(x + dx, X)).wait_send()

    for j in range(HZ):
        for h_ in range(H):

            @pl.when(jnp.logical_not((HZ * core + j == z) & (zh == h_)))
            def _(j=j, h_=h_):
                gz_copy(j, h_, zh, z).wait_send()

    def rest_left(k, _):
        y_ = lax.rem(y + k, Y)
        sy = around(y - k, Y)
        gc_copy(k, y_).wait_send()
        wc_copy(0, k, sy, x, core).wait_send()
        for dx in range(1, X):
            wc_copy(dx, k, sy, around(x - dx, X), core).wait_send()
            wx_copy(dx, k, sy, x, lax.rem(x + dx, X)).wait_send()
            gx_copy(dx, k, y_, lax.rem(x + dx, X)).wait_send()
        return 0

    lax.fori_loop(0, Y, rest_left, 0)

    def y_left(k, _):
        wy_copy(k, y, lax.rem(y + k, Y)).wait_send()
        gy_copy(k, lax.rem(y + k, Y)).wait_send()
        return 0

    lax.fori_loop(1, Y, y_left, 0)
    for copy in leaving:
        copy.wait()


def deliver(*refs):
    sources, targets, held, sems = refs[:3], refs[3:6], refs[6:9], refs[9]
    inward = [pltpu.make_async_copy(sources[n], held[n], sems.at[n]) for n in range(3)]
    outward = [pltpu.make_async_copy(held[n], targets[n], sems.at[n + 3]) for n in range(3)]
    for copy in inward:
        copy.start()
    for n in range(3):
        inward[n].wait()
        outward[n].start()
    for copy in outward:
        copy.wait()


def dp_count(sizes):
    return sizes[0] * sizes[1] * 2


def on_device(sizes, loader_rows, dest_list, row_counts, bucket_ids, conv_weight, out_grad):
    X, H, Y, Z = sizes
    HZ = Z // 2
    peers = Y * Z
    load, channels = loader_rows.shape[1:]
    pixels, out_width = out_grad.shape[1:]
    chunks = channels // LANES
    block = (load // peers + 1) * chunks
    rows_w = conv_weight.shape[0] // 2
    vmem = pltpu.VMEM
    sem = pltpu.SemaphoreType.DMA
    part = (HZ, rows_w, LANES)
    scratch = [
        vmem((load, channels), BF16),
        vmem((1, load), I32),
        vmem((1, 1), I32),
        vmem((1, 1), I32),
        vmem((pixels, out_width), BF16),
        vmem((pixels, out_width), F32),
        vmem((pixels, out_width), BF16),
        vmem((pixels, channels), BF16),
        vmem((2, rows_w, out_width), F32),
        vmem((peers * block, LANES), F32),
        vmem((peers, block, LANES), BF16),
        vmem((peers, block, LANES), BF16),
        vmem((X, peers, rows_w, LANES), BF16),
        vmem((TAPS, pixels, pixels), BF16),
        vmem((TAPS, pixels, out_width), BF16),
        vmem((pixels, channels), F32),
        vmem((8, channels), F32),
        vmem((pixels, channels), BF16),
        vmem((channels, pixels), BF16),
        vmem((pixels, channels), F32),
        vmem((TAPS * channels, out_width), F32),
        vmem((Y, HZ, 2, rows_w, out_width), BF16),
        vmem((Y, HZ, 2, rows_w, out_width), BF16),
        vmem((X, Y, *part), BF16),
        vmem((Y, *part), F32),
        vmem((X, Y, *part), BF16),
        vmem((Y, *part), BF16),
        vmem(part, F32),
        vmem((Y, *part), BF16),
        vmem(part, F32),
        vmem((H, Z, rows_w, LANES), F32),
        vmem((X, rows_w, LANES), F32),
        sem((5,)), sem((3,)), sem,
        sem((peers,)), sem((peers,)),
        sem((Z,)), sem((Z,)),
        sem((Y,)), sem((Y,)),
        sem((X, Y)), sem((X, Y)),
        sem((X, Y)), sem((X, Y)),
        sem((Y,)), sem((Y,)),
        sem((X, Y)), sem((X, Y)),
        sem((Y,)), sem((Y,)),
        sem((HZ, H)), sem((H, Z)),
        sem((X, 2)), sem((X,)),
    ]
    anywhere = pl.BlockSpec(memory_space=pl.ANY)
    flops = 2 * pixels * out_width * channels * TAPS * 3
    section, igrad, cgrad = pl.pallas_call(
        functools.partial(kernel, sizes),
        out_shape=(
            jax.ShapeDtypeStruct((pixels, out_width), BF16),
            jax.ShapeDtypeStruct((pixels, channels), BF16),
            jax.ShapeDtypeStruct((2, rows_w, out_width), F32),
        ),
        in_specs=[anywhere] * 6,
        out_specs=(anywhere,) * 3,
        scratch_shapes=scratch,
        compiler_params=pltpu.CompilerParams(
            collective_id=0, has_side_effects=True, vmem_limit_bytes=60 * 2**20
        ),
        cost_estimate=pl.CostEstimate(flops=flops, bytes_accessed=2**21, transcendentals=0),
        name="residual_section",
    )(
        loader_rows[0],
        dest_list,
        row_counts,
        bucket_ids,
        conv_weight.reshape(2, rows_w, out_width),
        out_grad[0],
    )
    section, igrad, cgrad = pl.pallas_call(
        deliver,
        out_shape=tuple(jax.ShapeDtypeStruct(a.shape, a.dtype) for a in (section, igrad, cgrad)),
        in_specs=[anywhere] * 3,
        out_specs=(anywhere,) * 3,
        scratch_shapes=[*(vmem(a.shape, a.dtype) for a in (section, igrad, cgrad)), sem((6,))],
        name="deliver",
    )(section, igrad, cgrad)
    return section[None], igrad[None], cgrad.reshape(conv_weight.shape)


def solution(mesh):
    sizes = layout(mesh)
    in_specs = (
        P("dp", "fsdp", None),
        P("dp", "fsdp"),
        P("dp", "fsdp"),
        P("dp", "fsdp"),
        P("fsdp", None),
        P("dp", "fsdp", None),
    )
    out_specs = (P("dp", "fsdp", None), P("dp", "fsdp", None), P("fsdp", None))
    return jax.shard_map(
        functools.partial(on_device, sizes), mesh=mesh, in_specs=in_specs, out_specs=out_specs, check_vma=False
    )
```

```python
import functools

import jax
import jax.numpy as jnp
from jax import lax
from jax.experimental import pallas as pl
from jax.experimental.pallas import tpu as pltpu
from jax.sharding import PartitionSpec as P

GROUPS = 32
TAPS = 9
LANES = 128
MESH = pl.DeviceIdType.MESH
BF16 = jnp.bfloat16
F32 = jnp.float32
I32 = jnp.int32


def layout(mesh):
    dp, fsdp = mesh.shape["dp"], mesh.shape["fsdp"]
    across, height = (4, 2), 8
    if fsdp % height:
        height = 3
    if dp % 16:
        across = (4, 1)
    return across[0], across[1], height, fsdp // height


def dot(a, b, dims=((1,), (0,))):
    return lax.dot_general(a, b, (dims, ((), ())), preferred_element_type=F32)


def iota(shape, dim):
    return lax.broadcasted_iota(I32, shape, dim)


def group_total(row, size):
    width = row.shape[1]
    lane = iota(row.shape, 1)
    step = 1
    while step < size:
        up = pltpu.roll(row, width - step, 1)
        down = pltpu.roll(row, step, 1)
        row = row + jnp.where((lane & step) == 0, up, down)
        step *= 2
    return row


def column_sum(values):
    total = jnp.sum(values, axis=0, keepdims=True)
    return jnp.broadcast_to(total, (8, values.shape[1]))


def kernel(
    sizes,
    slots_hbm, dest_hbm, count_hbm, bucket_hbm, shard_ref, grad_hbm,
    section_hbm, igrad_hbm, cgrad_hbm,
    slots_ref, dest_ref, count_ref, bucket_ref, grad_ref, section_ref, section_out, igrad_ref, cgrad_ref,
    wide, send, recv, weight, shifts, gcols, xhat_ref, rstd_ref, hidden_ref, hidden_t, hgrad,
    wgrad, core_out, core_in, x_out, x_own, x_in, y_out, y_own, y_in, z_out, z_in, quarters,
    in_sem, out_sem, local_sem, a2a_s, a2a_r, wz_s, wz_r, wy_s, wy_r, wx_s, wx_r, wc_s, wc_r,
    gc_s, gc_r, gx_s, gx_r, gy_s, gy_r, gz_s, gz_r, gf_s, gf_r,
):
    X, H, Y, Z = sizes
    HZ = Z // 2
    peers = Y * Z
    load, channels = slots_ref.shape
    pixels, out_width = grad_ref.shape
    chunks = channels // LANES
    cap = load // peers
    block = (cap + 1) * chunks
    rows_w = weight.shape[2]
    dp = lax.axis_index("dp")
    me = lax.axis_index("fsdp")
    core = lax.rem(dp, 2)
    zh = lax.rem(lax.div(dp, 2), H)
    x = lax.div(dp, 2 * H)
    y = lax.div(me, Z)
    z = lax.rem(me, Z)
    active = lax.div(z, HZ) == core

    def dp_at(x_, zh_, core_):
        return (x_ * H + zh_) * 2 + core_

    def around(value, extent):
        return lax.rem(value + extent, extent)

    arriving = [
        pltpu.make_async_copy(src, dst, in_sem.at[n])
        for n, (src, dst) in enumerate(
            (
                (dest_hbm, dest_ref),
                (count_hbm, count_ref),
                (slots_hbm, slots_ref),
                (bucket_hbm, bucket_ref),
                (grad_hbm, grad_ref),
            )
        )
    ]
    for copy in arriving:
        copy.start()
    lanes = pl.ds(pl.multiple_of(lax.rem(x, 2) * LANES, LANES), LANES)
    own_piece = pltpu.make_async_copy(shard_ref.at[lax.div(x, 2), :, lanes], weight.at[x, me], local_sem)

    @pl.when(active)
    def _():
        own_piece.start()

    barrier = pltpu.get_barrier_semaphore()

    def greet(dp_, fsdp_):
        pl.semaphore_signal(barrier, inc=1, device_id=(dp_, fsdp_), device_id_type=MESH)

    def greet_plane(k, _):
        greet(dp, lax.rem(me + k, peers))
        return 0

    lax.fori_loop(1, peers, greet_plane, 0)
    for dx in range(1, X):
        for other in range(2):
            greet(dp_at(lax.rem(x + dx, X), zh, other), me)
    greet(dp_at(x, zh, 1 - core), me)
    for dh in range(1, H):
        for tz in range(Z):
            greet(dp_at(x, lax.rem(zh + dh, H), core), y * Z + tz)
    greeted = peers - 1 + 2 * (X - 1) + 1 + (H - 1) * Z

    for copy in arriving:
        copy.wait()
    dest = dest_ref[...]
    usable = iota(dest.shape, 1) < count_ref[...]
    owner = jnp.where(usable, lax.div(dest, pixels), -1)
    place = lax.rem(dest, pixels)
    owns = iota((peers, load), 0) == owner
    owns_f = jnp.where(owns, 1.0, 0.0)
    before = jnp.where(iota((load, load), 0) < iota((load, load), 1), 1.0, 0.0).astype(BF16)
    earlier = dot(owns_f.astype(BF16), before)
    rank = jnp.sum(owns_f * earlier, axis=0, keepdims=True).astype(I32)
    slot = jnp.where(usable, owner * (cap + 1) + rank, -1)
    rows_all = peers * (cap + 1)
    pick = jnp.where(iota((rows_all, load), 0) == slot, 1.0, 0.0).astype(BF16)
    packed = dot(pick, slots_ref[...])
    for c in range(chunks):
        wide[pl.ds(c, rows_all, stride=chunks), :] = packed[:, c * LANES : (c + 1) * LANES]
    marks = jnp.where(
        iota((LANES, load), 0) == rank, (place - pixels).astype(F32), 0.0
    ).astype(BF16)
    places = dot(owns_f.astype(BF16), marks, ((1,), (1,))) + float(pixels)
    wide[pl.ds(cap * chunks, peers, stride=block), :] = places
    send[...] = wide[...].astype(BF16).reshape(send.shape)

    pl.semaphore_wait(barrier, greeted)

    def remote(src, dst, s_sem, r_sem, where):
        return pltpu.make_async_remote_copy(
            src_ref=src, dst_ref=dst, send_sem=s_sem, recv_sem=r_sem, device_id=where, device_id_type=MESH
        )

    def w_quarter(b, x_):
        return weight.at[x_, b]

    def w_chunk(y_, x_, core_):
        return weight.at[x_, pl.ds(Z * y_ + HZ * core_, HZ)]

    def wz_copy(dz, target, b):
        part = w_quarter(b, x)
        return remote(part, part, wz_s.at[dz], wz_r.at[dz], (dp, y * Z + target))

    def wy_copy(k, y_src, y_dst):
        part = w_chunk(y_src, x, core)
        return remote(part, part, wy_s.at[k], wy_r.at[k], (dp, y_dst * Z + z))

    def wx_copy(dx, k, y_, x_src, x_dst):
        part = w_chunk(y_, x_src, core)
        return remote(part, part, wx_s.at[dx, k], wx_r.at[dx, k], (dp_at(x_dst, zh, core), me))

    def wc_copy(dx, k, y_, x_src, core_):
        part = w_chunk(y_, x_src, core_)
        return remote(part, part, wc_s.at[dx, k], wc_r.at[dx, k], (dp_at(x, zh, 1 - core), me))

    def a2a_copy(k, source, target):
        return remote(send.at[target], recv.at[source], a2a_s.at[k], a2a_r.at[k], (dp, target))

    def a2a_peer(k, sign):
        ty = around(y + sign * lax.div(k, Z), Y)
        tz = around(z + sign * lax.rem(k, Z), Z)
        return ty * Z + tz

    @pl.when(active)
    def _():
        own_piece.wait()
        for dz in range(1, Z):
            wz_copy(dz, around(z + dz, Z), me).start()

    def a2a_start(k, _):
        a2a_copy(k, me, a2a_peer(k, 1)).start()
        return 0

    lax.fori_loop(1, peers, a2a_start, 0)
    recv[me] = send[me]

    bucket = bucket_ref[...]
    width = jnp.where(bucket == 0, 8, jnp.where(bucket == 1, 16, 32))
    grad = grad_ref[...]
    pixel = iota((pixels, pixels), 0)
    gap = iota((pixels, pixels), 1) - pixel
    column = pixel & (width - 1)

    def make_shift(t, _):
        a = lax.div(t, 3) - 1
        b = lax.rem(t, 3) - 1
        near = column + b
        hit = (gap == a * width + b) & (near >= 0) & (near < width)
        shift = jnp.where(hit, 1.0, 0.0).astype(BF16)
        shifts[t] = shift
        gcols[TAPS - 1 - t] = dot(shift, grad).astype(BF16)
        return 0

    lax.fori_loop(0, TAPS, make_shift, 0, unroll=3)

    for j in range(HZ):
        sz = HZ * core + j

        @pl.when(sz != z)
        def _(sz=sz):
            wz_copy(around(z - sz, Z), z, y * Z + sz).wait_recv()

    for dy in range(1, Y):
        wy_copy(dy, y, lax.rem(y + dy, Y)).start()

    def w_forward(k, _):
        sy = around(y - k, Y)

        @pl.when(k > 0)
        def _():
            wy_copy(k, sy, y).wait_recv()

        for dx in range(1, X):
            wx_copy(dx, k, sy, x, lax.rem(x + dx, X)).start()
        wc_copy(0, k, sy, x, core).start()
        return 0

    lax.fori_loop(0, Y, w_forward, 0)

    def a2a_wait(k, _):
        a2a_copy(k, a2a_peer(k, -1), me).wait_recv()
        return 0

    lax.fori_loop(1, peers, a2a_wait, 0)
    wide[...] = recv[...].astype(F32).reshape(wide.shape)
    got_places = wide[pl.ds(cap * chunks, peers, stride=block), :].astype(BF16)
    index = iota((peers, rows_all), 1)
    spread = jnp.where(lax.div(index, cap + 1) == iota((peers, rows_all), 0), 1.0, 0.0).astype(BF16)
    by_rank = dot(got_places, spread, ((0,), (0,)))
    index = iota((LANES, rows_all), 1)
    fits = lax.rem(index, cap + 1) == iota((LANES, rows_all), 0)
    where_to = jnp.sum(jnp.where(fits, by_rank, 0.0), axis=0, keepdims=True).astype(I32)
    put = jnp.where(iota((pixels, rows_all), 0) == where_to, 1.0, 0.0).astype(BF16)
    features = jnp.concatenate(
        [dot(put, wide[pl.ds(c, rows_all, stride=chunks), :].astype(BF16)) for c in range(chunks)], axis=1
    )
    per_group = channels // GROUPS
    share = 1.0 / float(pixels * per_group)
    centre = group_total(column_sum(features), per_group) * share
    centred = features - centre[:1]
    spread_of = group_total(column_sum(centred * centred), per_group) * share
    rstd = lax.rsqrt(spread_of + 1e-05)
    xhat = centred * rstd[:1]
    hidden = xhat * jax.nn.sigmoid(xhat)
    rstd_ref[...] = rstd
    xhat_ref[...] = xhat
    hidden_t[...] = hidden.T.astype(BF16)
    hidden_ref[...] = hidden.astype(BF16)
    section_ref[...] = features[:, :out_width]

    def w_term(t, _):
        wgrad[pl.ds(pl.multiple_of(t * channels, channels), channels), :] = dot(hidden_t[...], gcols[t])
        return 0

    lax.fori_loop(0, TAPS, w_term, 0, unroll=True)

    rows_b = 2 * rows_w
    span = HZ * rows_b

    def my_rows(y_, core_):
        return pl.ds(pl.multiple_of((Z * y_ + HZ * core_) * rows_b, rows_b), span)

    def gc_copy(k, y_):
        return remote(core_out.at[y_], core_in.at[y_], gc_s.at[k], gc_r.at[k], (dp_at(x, zh, 1 - core), me))

    def gx_copy(dx, k, y_, x_):
        return remote(x_out.at[x_, y_], x_in.at[dx, y_], gx_s.at[dx, k], gx_r.at[dx, k], (dp_at(x_, zh, core), me))

    def gy_copy(k, y_):
        return remote(y_out.at[k], y_in.at[k], gy_s.at[k], gy_r.at[k], (dp, y_ * Z + z))

    def farthest_first(i):
        odd = lax.rem(i, 2)
        return Y // 2 + lax.div(i, 2) * (1 - odd) - lax.div(i + 1, 2) * odd

    far_x = sorted(range(1, X), key=lambda dx: -min(dx, X - dx))

    def core_stage(i, _):
        k = farthest_first(i)
        y_ = lax.rem(y + k, Y)
        core_out[y_] = wgrad[my_rows(y_, 1 - core), :].astype(BF16).reshape(core_out.shape[1:])
        gc_copy(k, y_).start()
        return 0

    lax.fori_loop(0, Y, core_stage, 0)

    def x_stage(i, _):
        k = farthest_first(i)
        y_ = lax.rem(y + k, Y)
        gc_copy(k, y_).wait_recv()
        both = wgrad[my_rows(y_, core), :].reshape(core_in.shape[1:]) + core_in[y_].astype(F32)
        own = None
        for x_ in range(X):
            first = (x_ % 2) * LANES
            part = both[:, x_ // 2, :, first : first + LANES]
            x_out[x_, y_] = part.astype(BF16)
            own = part if own is None else jnp.where(x == x_, part, own)
        x_own[y_] = own
        for dx in far_x:
            gx_copy(dx, k, y_, lax.rem(x + dx, X)).start()
        return 0

    lax.fori_loop(0, Y, x_stage, 0)

    def w_cross(k, _):
        sy = around(y - k, Y)
        for dx in range(1, X):
            sx = around(x - dx, X)
            wx_copy(dx, k, sy, sx, x).wait_recv()
            wc_copy(dx, k, sy, sx, core).start()
        return 0

    lax.fori_loop(0, Y, w_cross, 0)

    def x_total(k, y_):
        total = x_own[y_]
        for dx in range(1, X):
            gx_copy(dx, k, y_, x).wait_recv()
            total = total + x_in[dx, y_].astype(F32)
        return total

    def y_stage(i, _):
        k = farthest_first(i)
        y_ = lax.rem(y + k, Y)
        total = x_total(k, y_)

        @pl.when(k == 0)
        def _():
            y_own[...] = total

        @pl.when(k > 0)
        def _():
            y_out[k] = total.astype(BF16)
            gy_copy(k, y_).start()

        return 0

    lax.fori_loop(0, Y, y_stage, 0)

    def w_last(k, _):
        sy = around(y - k, Y)
        for dx in range(X):
            wc_copy(dx, k, sy, around(x - dx, X), 1 - core).wait_recv()
        return 0

    lax.fori_loop(0, Y, w_last, 0)
    hgrad[...] = jnp.zeros_like(hgrad)
    taps_row = 3
    blocks_row = taps_row * channels // (2 * rows_w)

    def conv_row(i, _):
        blocks = pl.ds(i * blocks_row, blocks_row)
        halves = [
            jnp.stack([weight[2 * r + h, blocks] for r in range(2)], axis=1).reshape(taps_row * channels, LANES)
            for h in range(2)
        ]
        kernel_row = jnp.concatenate(halves, axis=1)
        for j in range(taps_row):
            t = i * taps_row + j
            tap = kernel_row[j * channels : (j + 1) * channels]
            hgrad[...] += dot(gcols[t], tap, ((1,), (1,)))
            near = dot(shifts[t], hidden_ref[...]).astype(BF16)
            section_ref[...] += dot(near, tap)
        return 0

    lax.fori_loop(0, TAPS // taps_row, conv_row, 0)
    section_out[...] = section_ref[...].astype(BF16)
    xhat = xhat_ref[...]
    gate = jax.nn.sigmoid(xhat)
    slope = hgrad[...] * (gate * (1.0 + xhat * (1.0 - gate)))
    mean_s = group_total(column_sum(slope), per_group) * share
    mean_sx = group_total(column_sum(slope * xhat), per_group) * share
    back = rstd_ref[:1, :] * (slope - mean_s[:1] - xhat * mean_sx[:1])
    igrad_ref[:, :out_width] = (back[:, :out_width] + grad_ref[...].astype(F32)).astype(BF16)
    igrad_ref[:, out_width:] = back[:, out_width:].astype(BF16)
    leaving = [
        pltpu.make_async_copy(src, dst, out_sem.at[n])
        for n, (src, dst) in enumerate(
            ((section_out, section_hbm), (igrad_ref, igrad_hbm), (cgrad_ref, cgrad_hbm))
        )
    ]
    leaving[0].start()
    leaving[1].start()

    def y_add(k, _):
        gy_copy(k, y).wait_recv()
        y_own[...] += y_in[k].astype(F32)
        return 0

    lax.fori_loop(1, Y, y_add, 0)
    z_out[...] = y_own[...]

    def gz_copy(j, dh, h_, sh, sz):
        where = (dp_at(x, h_, core), y * Z + HZ * core + j)
        return remote(z_out.at[j], z_in.at[sh, sz], gz_s.at[j, dh], gz_r.at[sh, sz], where)

    for dh in (*range(1, H), 0):
        h_ = lax.rem(zh + dh, H)
        for j in range(HZ):
            if dh:
                gz_copy(j, dh, h_, zh, z).start()
                continue
            mine = HZ * core + j == z

            @pl.when(mine)
            def _(j=j):
                z_in[zh, z] = z_out[j]

            @pl.when(jnp.logical_not(mine))
            def _(j=j, h_=h_):
                gz_copy(j, 0, h_, zh, z).start()

    def gf_copy(dx, core_, x_src, x_dst):
        return remote(quarters.at[x_src], quarters.at[x_src], gf_s.at[dx, core_], gf_r.at[x_src], (dp_at(x_dst, zh, core_), me))

    images = peers * dp_count(sizes)
    scale = 1.0 / float(images * pixels) ** 0.5

    @pl.when(active)
    def _():
        for h_ in range(H):
            for sz in range(Z):

                @pl.when(jnp.logical_not((zh == h_) & (z == sz)))
                def _(h_=h_, sz=sz):
                    gz_copy(0, 0, zh, h_, sz).wait_recv()

        total = z_in[0, 0]
        for h_ in range(H):
            for sz in range(Z):
                if h_ or sz:
                    total = total + z_in[h_, sz]
        quarters[x] = total * scale
        for dx in far_x:
            for other in range(2):
                gf_copy(dx, other, x, lax.rem(x + dx, X)).start()
        gf_copy(0, 1 - core, x, x).start()

    for x_ in range(X):

        @pl.when(jnp.logical_not(active & (x == x_)))
        def _(x_=x_):
            gf_copy(0, 0, x_, x).wait_recv()

    for x_ in range(X):
        first = (x_ % 2) * LANES
        cgrad_ref[x_ // 2, :, first : first + LANES] = quarters[x_]
    leaving[2].start()

    def a2a_left(k, _):
        a2a_copy(k, me, a2a_peer(k, 1)).wait_send()
        return 0

    lax.fori_loop(1, peers, a2a_left, 0)

    @pl.when(active)
    def _():
        for dz in range(1, Z):
            wz_copy(dz, around(z + dz, Z), me).wait_send()
        gf_copy(0, 1 - core, x, x).wait_send()
        for dx in range(1, X):
            for other in range(2):
                gf_copy(dx, other, x, lax.rem(x + dx, X)).wait_send()

    for j in range(HZ):
        for dh in range(1, H):
            gz_copy(j, dh, lax.rem(zh + dh, H), zh, z).wait_send()

        @pl.when(HZ * core + j != z)
        def _(j=j):
            gz_copy(j, 0, zh, zh, z).wait_send()

    def rest_left(k, _):
        y_ = lax.rem(y + k, Y)
        sy = around(y - k, Y)
        gc_copy(k, y_).wait_send()
        wc_copy(0, k, sy, x, core).wait_send()
        for dx in range(1, X):
            wc_copy(dx, k, sy, around(x - dx, X), core).wait_send()
            wx_copy(dx, k, sy, x, lax.rem(x + dx, X)).wait_send()
            gx_copy(dx, k, y_, lax.rem(x + dx, X)).wait_send()
        return 0

    lax.fori_loop(0, Y, rest_left, 0)

    def y_left(k, _):
        wy_copy(k, y, lax.rem(y + k, Y)).wait_send()
        gy_copy(k, lax.rem(y + k, Y)).wait_send()
        return 0

    lax.fori_loop(1, Y, y_left, 0)
    for copy in leaving:
        copy.wait()


def deliver(*refs):
    sources, targets, held, sems = refs[:3], refs[3:6], refs[6:9], refs[9]
    inward = [pltpu.make_async_copy(sources[n], held[n], sems.at[n]) for n in range(3)]
    outward = [pltpu.make_async_copy(held[n], targets[n], sems.at[n + 3]) for n in range(3)]
    for copy in inward:
        copy.start()
    for n in range(3):
        inward[n].wait()
        outward[n].start()
    for copy in outward:
        copy.wait()


def dp_count(sizes):
    return sizes[0] * sizes[1] * 2


def on_device(sizes, loader_rows, dest_list, row_counts, bucket_ids, conv_weight, out_grad):
    X, H, Y, Z = sizes
    HZ = Z // 2
    peers = Y * Z
    load, channels = loader_rows.shape[1:]
    pixels, out_width = out_grad.shape[1:]
    chunks = channels // LANES
    block = (load // peers + 1) * chunks
    rows_w = conv_weight.shape[0] // 2
    vmem = pltpu.VMEM
    sem = pltpu.SemaphoreType.DMA
    part = (HZ, rows_w, LANES)
    scratch = [
        vmem((load, channels), BF16),
        vmem((1, load), I32),
        vmem((1, 1), I32),
        vmem((1, 1), I32),
        vmem((pixels, out_width), BF16),
        vmem((pixels, out_width), F32),
        vmem((pixels, out_width), BF16),
        vmem((pixels, channels), BF16),
        vmem((2, rows_w, out_width), F32),
        vmem((peers * block, LANES), F32),
        vmem((peers, block, LANES), BF16),
        vmem((peers, block, LANES), BF16),
        vmem((X, peers, rows_w, LANES), BF16),
        vmem((TAPS, pixels, pixels), BF16),
        vmem((TAPS, pixels, out_width), BF16),
        vmem((pixels, channels), F32),
        vmem((8, channels), F32),
        vmem((pixels, channels), BF16),
        vmem((channels, pixels), BF16),
        vmem((pixels, channels), F32),
        vmem((TAPS * channels, out_width), F32),
        vmem((Y, HZ, 2, rows_w, out_width), BF16),
        vmem((Y, HZ, 2, rows_w, out_width), BF16),
        vmem((X, Y, *part), BF16),
        vmem((Y, *part), F32),
        vmem((X, Y, *part), BF16),
        vmem((Y, *part), BF16),
        vmem(part, F32),
        vmem((Y, *part), BF16),
        vmem(part, F32),
        vmem((H, Z, rows_w, LANES), F32),
        vmem((X, rows_w, LANES), F32),
        sem((5,)), sem((3,)), sem,
        sem((peers,)), sem((peers,)),
        sem((Z,)), sem((Z,)),
        sem((Y,)), sem((Y,)),
        sem((X, Y)), sem((X, Y)),
        sem((X, Y)), sem((X, Y)),
        sem((Y,)), sem((Y,)),
        sem((X, Y)), sem((X, Y)),
        sem((Y,)), sem((Y,)),
        sem((HZ, H)), sem((H, Z)),
        sem((X, 2)), sem((X,)),
    ]
    anywhere = pl.BlockSpec(memory_space=pl.ANY)
    flops = 2 * pixels * out_width * channels * TAPS * 3
    section, igrad, cgrad = pl.pallas_call(
        functools.partial(kernel, sizes),
        out_shape=(
            jax.ShapeDtypeStruct((pixels, out_width), BF16),
            jax.ShapeDtypeStruct((pixels, channels), BF16),
            jax.ShapeDtypeStruct((2, rows_w, out_width), F32),
        ),
        in_specs=[anywhere] * 6,
        out_specs=(anywhere,) * 3,
        scratch_shapes=scratch,
        compiler_params=pltpu.CompilerParams(
            collective_id=0, has_side_effects=True, vmem_limit_bytes=60 * 2**20
        ),
        cost_estimate=pl.CostEstimate(flops=flops, bytes_accessed=2**21, transcendentals=0),
        name="residual_section",
    )(
        loader_rows[0],
        dest_list,
        row_counts,
        bucket_ids,
        conv_weight.reshape(2, rows_w, out_width),
        out_grad[0],
    )
    section, igrad, cgrad = pl.pallas_call(
        deliver,
        out_shape=tuple(jax.ShapeDtypeStruct(a.shape, a.dtype) for a in (section, igrad, cgrad)),
        in_specs=[anywhere] * 3,
        out_specs=(anywhere,) * 3,
        scratch_shapes=[*(vmem(a.shape, a.dtype) for a in (section, igrad, cgrad)), sem((6,))],
        name="deliver",
    )(section, igrad, cgrad)
    return section[None], igrad[None], cgrad.reshape(conv_weight.shape)


def solution(mesh):
    sizes = layout(mesh)
    in_specs = (
        P("dp", "fsdp", None),
        P("dp", "fsdp"),
        P("dp", "fsdp"),
        P("dp", "fsdp"),
        P("fsdp", None),
        P("dp", "fsdp", None),
    )
    out_specs = (P("dp", "fsdp", None), P("dp", "fsdp", None), P("fsdp", None))
    return jax.shard_map(
        functools.partial(on_device, sizes), mesh=mesh, in_specs=in_specs, out_specs=out_specs, check_vma=False
    )
```

```python
import functools

import jax
import jax.numpy as jnp
from jax import lax
from jax.experimental import pallas as pl
from jax.experimental.pallas import tpu as pltpu
from jax.sharding import PartitionSpec as P

GROUPS = 32
TAPS = 9
LANES = 128
MESH = pl.DeviceIdType.MESH
BF16 = jnp.bfloat16
F32 = jnp.float32
I32 = jnp.int32


def layout(mesh):
    dp, fsdp = mesh.shape["dp"], mesh.shape["fsdp"]
    across, height = (4, 2), 8
    if fsdp % height:
        height = 3
    if dp % 16:
        across = (4, 1)
    return across[0], across[1], height, fsdp // height


def dot(a, b, dims=((1,), (0,))):
    return lax.dot_general(a, b, (dims, ((), ())), preferred_element_type=F32)


def iota(shape, dim):
    return lax.broadcasted_iota(I32, shape, dim)


def group_total(row, size):
    width = row.shape[1]
    lane = iota(row.shape, 1)
    step = 1
    while step < size:
        up = pltpu.roll(row, width - step, 1)
        down = pltpu.roll(row, step, 1)
        row = row + jnp.where((lane & step) == 0, up, down)
        step *= 2
    return row


def column_sum(values):
    total = jnp.sum(values, axis=0, keepdims=True)
    return jnp.broadcast_to(total, (8, values.shape[1]))


def kernel(
    sizes,
    slots_hbm, dest_hbm, count_hbm, bucket_hbm, shard_ref, grad_hbm,
    section_hbm, igrad_hbm, cgrad_hbm,
    slots_ref, dest_ref, count_ref, bucket_ref, grad_ref, section_ref, section_out, igrad_ref, cgrad_ref,
    wide, send, recv, weight, shifts, gcols, xhat_ref, rstd_ref, hidden_ref, hidden_t, hgrad,
    wgrad, core_out, core_in, x_out, x_own, x_in, y_out, y_own, y_in, z_out, z_in, quarters,
    in_sem, out_sem, local_sem, a2a_s, a2a_r, wz_s, wz_r, wy_s, wy_r, wx_s, wx_r, wc_s, wc_r,
    gc_s, gc_r, gx_s, gx_r, gy_s, gy_r, gz_s, gz_r, gf_s, gf_r,
):
    X, H, Y, Z = sizes
    HZ = Z // 2
    peers = Y * Z
    load, channels = slots_ref.shape
    pixels, out_width = grad_ref.shape
    chunks = channels // LANES
    cap = load // peers
    block = (cap + 1) * chunks
    rows_w = weight.shape[2]
    dp = lax.axis_index("dp")
    me = lax.axis_index("fsdp")
    core = lax.rem(dp, 2)
    zh = lax.rem(lax.div(dp, 2), H)
    x = lax.div(dp, 2 * H)
    y = lax.div(me, Z)
    z = lax.rem(me, Z)
    active = lax.div(z, HZ) == core

    def dp_at(x_, zh_, core_):
        return (x_ * H + zh_) * 2 + core_

    def around(value, extent):
        return lax.rem(value + extent, extent)

    arriving = [
        pltpu.make_async_copy(src, dst, in_sem.at[n])
        for n, (src, dst) in enumerate(
            (
                (dest_hbm, dest_ref),
                (count_hbm, count_ref),
                (slots_hbm, slots_ref),
                (bucket_hbm, bucket_ref),
                (grad_hbm, grad_ref),
            )
        )
    ]
    for copy in arriving:
        copy.start()
    lanes = pl.ds(pl.multiple_of(lax.rem(x, 2) * LANES, LANES), LANES)
    own_piece = pltpu.make_async_copy(shard_ref.at[lax.div(x, 2), :, lanes], weight.at[x, me], local_sem)

    @pl.when(active)
    def _():
        own_piece.start()

    barrier = pltpu.get_barrier_semaphore()

    def greet(dp_, fsdp_):
        pl.semaphore_signal(barrier, inc=1, device_id=(dp_, fsdp_), device_id_type=MESH)

    def greet_plane(k, _):
        greet(dp, lax.rem(me + k, peers))
        return 0

    lax.fori_loop(1, peers, greet_plane, 0)
    for dx in range(1, X):
        for other in range(2):
            greet(dp_at(lax.rem(x + dx, X), zh, other), me)
    greet(dp_at(x, zh, 1 - core), me)
    for dh in range(1, H):
        for tz in range(Z):
            greet(dp_at(x, lax.rem(zh + dh, H), core), y * Z + tz)
    greeted = peers - 1 + 2 * (X - 1) + 1 + (H - 1) * Z

    for copy in arriving:
        copy.wait()
    dest = dest_ref[...]
    usable = iota(dest.shape, 1) < count_ref[...]
    owner = jnp.where(usable, lax.div(dest, pixels), -1)
    place = lax.rem(dest, pixels)
    owns = iota((peers, load), 0) == owner
    owns_f = jnp.where(owns, 1.0, 0.0)
    before = jnp.where(iota((load, load), 0) < iota((load, load), 1), 1.0, 0.0).astype(BF16)
    earlier = dot(owns_f.astype(BF16), before)
    rank = jnp.sum(owns_f * earlier, axis=0, keepdims=True).astype(I32)
    slot = jnp.where(usable, owner * (cap + 1) + rank, -1)
    rows_all = peers * (cap + 1)
    pick = jnp.where(iota((rows_all, load), 0) == slot, 1.0, 0.0).astype(BF16)
    packed = dot(pick, slots_ref[...])
    for c in range(chunks):
        wide[pl.ds(c, rows_all, stride=chunks), :] = packed[:, c * LANES : (c + 1) * LANES]
    marks = jnp.where(
        iota((LANES, load), 0) == rank, (place - pixels).astype(F32), 0.0
    ).astype(BF16)
    places = dot(owns_f.astype(BF16), marks, ((1,), (1,))) + float(pixels)
    wide[pl.ds(cap * chunks, peers, stride=block), :] = places
    send[...] = wide[...].astype(BF16).reshape(send.shape)

    pl.semaphore_wait(barrier, greeted)

    def remote(src, dst, s_sem, r_sem, where):
        return pltpu.make_async_remote_copy(
            src_ref=src, dst_ref=dst, send_sem=s_sem, recv_sem=r_sem, device_id=where, device_id_type=MESH
        )

    def w_quarter(b, x_):
        return weight.at[x_, b]

    def w_chunk(y_, x_, core_):
        return weight.at[x_, pl.ds(Z * y_ + HZ * core_, HZ)]

    def wz_copy(dz, target, b):
        part = w_quarter(b, x)
        return remote(part, part, wz_s.at[dz], wz_r.at[dz], (dp, y * Z + target))

    def wy_copy(k, y_src, y_dst):
        part = w_chunk(y_src, x, core)
        return remote(part, part, wy_s.at[k], wy_r.at[k], (dp, y_dst * Z + z))

    def wx_copy(dx, k, y_, x_src, x_dst):
        part = w_chunk(y_, x_src, core)
        return remote(part, part, wx_s.at[dx, k], wx_r.at[dx, k], (dp_at(x_dst, zh, core), me))

    def wc_copy(dx, k, y_, x_src, core_):
        part = w_chunk(y_, x_src, core_)
        return remote(part, part, wc_s.at[dx, k], wc_r.at[dx, k], (dp_at(x, zh, 1 - core), me))

    def a2a_copy(k, source, target):
        return remote(send.at[target], recv.at[source], a2a_s.at[k], a2a_r.at[k], (dp, target))

    def a2a_peer(k, sign):
        ty = around(y + sign * lax.div(k, Z), Y)
        tz = around(z + sign * lax.rem(k, Z), Z)
        return ty * Z + tz

    @pl.when(active)
    def _():
        own_piece.wait()
        for dz in range(1, Z):
            wz_copy(dz, around(z + dz, Z), me).start()

    def a2a_start(k, _):
        a2a_copy(k, me, a2a_peer(k, 1)).start()
        return 0

    lax.fori_loop(1, peers, a2a_start, 0)
    recv[me] = send[me]

    bucket = bucket_ref[...]
    width = jnp.where(bucket == 0, 8, jnp.where(bucket == 1, 16, 32))
    grad = grad_ref[...]
    pixel = iota((pixels, pixels), 0)
    gap = iota((pixels, pixels), 1) - pixel
    column = pixel & (width - 1)

    def make_shift(t, _):
        a = lax.div(t, 3) - 1
        b = lax.rem(t, 3) - 1
        near = column + b
        hit = (gap == a * width + b) & (near >= 0) & (near < width)
        shift = jnp.where(hit, 1.0, 0.0).astype(BF16)
        shifts[t] = shift
        gcols[TAPS - 1 - t] = dot(shift, grad).astype(BF16)
        return 0

    lax.fori_loop(0, TAPS, make_shift, 0, unroll=3)

    for j in range(HZ):
        sz = HZ * core + j

        @pl.when(sz != z)
        def _(sz=sz):
            wz_copy(around(z - sz, Z), z, y * Z + sz).wait_recv()

    for dy in range(1, Y):
        wy_copy(dy, y, lax.rem(y + dy, Y)).start()

    def w_forward(k, _):
        sy = around(y - k, Y)

        @pl.when(k > 0)
        def _():
            wy_copy(k, sy, y).wait_recv()

        for dx in range(1, X):
            wx_copy(dx, k, sy, x, lax.rem(x + dx, X)).start()
        wc_copy(0, k, sy, x, core).start()
        return 0

    lax.fori_loop(0, Y, w_forward, 0)

    def a2a_wait(k, _):
        a2a_copy(k, a2a_peer(k, -1), me).wait_recv()
        return 0

    lax.fori_loop(1, peers, a2a_wait, 0)
    wide[...] = recv[...].astype(F32).reshape(wide.shape)
    got_places = wide[pl.ds(cap * chunks, peers, stride=block), :].astype(BF16)
    index = iota((peers, rows_all), 1)
    spread = jnp.where(lax.div(index, cap + 1) == iota((peers, rows_all), 0), 1.0, 0.0).astype(BF16)
    by_rank = dot(got_places, spread, ((0,), (0,)))
    index = iota((LANES, rows_all), 1)
    fits = lax.rem(index, cap + 1) == iota((LANES, rows_all), 0)
    where_to = jnp.sum(jnp.where(fits, by_rank, 0.0), axis=0, keepdims=True).astype(I32)
    put = jnp.where(iota((pixels, rows_all), 0) == where_to, 1.0, 0.0).astype(BF16)
    features = jnp.concatenate(
        [dot(put, wide[pl.ds(c, rows_all, stride=chunks), :].astype(BF16)) for c in range(chunks)], axis=1
    )
    per_group = channels // GROUPS
    share = 1.0 / float(pixels * per_group)
    centre = group_total(column_sum(features), per_group) * share
    centred = features - centre[:1]
    spread_of = group_total(column_sum(centred * centred), per_group) * share
    rstd = lax.rsqrt(spread_of + 1e-05)
    xhat = centred * rstd[:1]
    hidden = xhat * jax.nn.sigmoid(xhat)
    rstd_ref[...] = rstd
    xhat_ref[...] = xhat
    hidden_t[...] = hidden.T.astype(BF16)
    hidden_ref[...] = hidden.astype(BF16)
    section_ref[...] = features[:, :out_width]

    rows_b = 2 * rows_w
    span = HZ * rows_b

    def my_rows(y_, core_):
        return pl.ds(pl.multiple_of((Z * y_ + HZ * core_) * rows_b, rows_b), span)

    def gc_copy(k, y_):
        return remote(core_out.at[y_], core_in.at[y_], gc_s.at[k], gc_r.at[k], (dp_at(x, zh, 1 - core), me))

    def gx_copy(dx, k, y_, x_):
        return remote(x_out.at[x_, y_], x_in.at[dx, y_], gx_s.at[dx, k], gx_r.at[dx, k], (dp_at(x_, zh, core), me))

    def gy_copy(k, y_):
        return remote(y_out.at[k], y_in.at[k], gy_s.at[k], gy_r.at[k], (dp, y_ * Z + z))

    far_x = sorted(range(1, X), key=lambda dx: -min(dx, X - dx))

    rows_y = Z * rows_b
    taps_y = -(-rows_y // channels)

    def piece(i):
        return lax.rem(i + 1, Y)

    def w_term(t):
        wgrad[pl.ds(pl.multiple_of(t * channels, channels), channels), :] = dot(hidden_t[...], gcols[t])

    def core_stage(i, _):
        k = piece(i)
        y_ = lax.rem(y + k, Y)
        first = lax.div(y_ * rows_y, channels)
        if rows_y % channels:
            @pl.when((i == 0) | (y_ == 0))
            def _():
                w_term(first)
        else:
            w_term(first)
        for later in range(1, taps_y):
            w_term(first + later)
        core_out[y_] = wgrad[my_rows(y_, 1 - core), :].astype(BF16).reshape(core_out.shape[1:])
        gc_copy(k, y_).start()
        return 0

    def x_stage(i, _):
        k = piece(i)
        y_ = lax.rem(y + k, Y)
        gc_copy(k, y_).wait_recv()
        both = wgrad[my_rows(y_, core), :].reshape(core_in.shape[1:]) + core_in[y_].astype(F32)
        own = None
        for x_ in range(X):
            first = (x_ % 2) * LANES
            part = both[:, x_ // 2, :, first : first + LANES]
            x_out[x_, y_] = part.astype(BF16)
            own = part if own is None else jnp.where(x == x_, part, own)
        x_own[y_] = own
        for dx in far_x:
            gx_copy(dx, k, y_, lax.rem(x + dx, X)).start()
        return 0

    def both_stages(i, _):
        core_stage(i + lag, 0)
        x_stage(i, 0)
        return 0

    lag = 2
    lax.fori_loop(0, lag, core_stage, 0)
    lax.fori_loop(0, Y - lag, both_stages, 0)
    lax.fori_loop(Y - lag, Y, x_stage, 0)

    def w_cross(k, _):
        sy = around(y - k, Y)
        for dx in range(1, X):
            sx = around(x - dx, X)
            wx_copy(dx, k, sy, sx, x).wait_recv()
            wc_copy(dx, k, sy, sx, core).start()
        return 0

    lax.fori_loop(0, Y, w_cross, 0)

    def x_total(k, y_):
        total = x_own[y_]
        for dx in range(1, X):
            gx_copy(dx, k, y_, x).wait_recv()
            total = total + x_in[dx, y_].astype(F32)
        return total

    def y_stage(i, _):
        k = piece(i)
        y_ = lax.rem(y + k, Y)
        total = x_total(k, y_)

        @pl.when(k == 0)
        def _():
            y_own[...] = total

        @pl.when(k > 0)
        def _():
            y_out[k] = total.astype(BF16)
            gy_copy(k, y_).start()

        return 0

    lax.fori_loop(0, Y, y_stage, 0)

    def w_last(k, _):
        sy = around(y - k, Y)
        for dx in range(X):
            wc_copy(dx, k, sy, around(x - dx, X), 1 - core).wait_recv()
        return 0

    lax.fori_loop(0, Y, w_last, 0)
    hgrad[...] = jnp.zeros_like(hgrad)
    taps_row = 3
    blocks_row = taps_row * channels // (2 * rows_w)

    def conv_row(i, _):
        blocks = pl.ds(i * blocks_row, blocks_row)
        halves = [
            jnp.stack([weight[2 * r + h, blocks] for r in range(2)], axis=1).reshape(taps_row * channels, LANES)
            for h in range(2)
        ]
        kernel_row = jnp.concatenate(halves, axis=1)
        for j in range(taps_row):
            t = i * taps_row + j
            tap = kernel_row[j * channels : (j + 1) * channels]
            hgrad[...] += dot(gcols[t], tap, ((1,), (1,)))
            near = dot(shifts[t], hidden_ref[...]).astype(BF16)
            section_ref[...] += dot(near, tap)
        return 0

    lax.fori_loop(0, TAPS // taps_row, conv_row, 0)
    section_out[...] = section_ref[...].astype(BF16)
    xhat = xhat_ref[...]
    gate = jax.nn.sigmoid(xhat)
    slope = hgrad[...] * (gate * (1.0 + xhat * (1.0 - gate)))
    mean_s = group_total(column_sum(slope), per_group) * share
    mean_sx = group_total(column_sum(slope * xhat), per_group) * share
    back = rstd_ref[:1, :] * (slope - mean_s[:1] - xhat * mean_sx[:1])
    igrad_ref[:, :out_width] = (back[:, :out_width] + grad_ref[...].astype(F32)).astype(BF16)
    igrad_ref[:, out_width:] = back[:, out_width:].astype(BF16)
    leaving = [
        pltpu.make_async_copy(src, dst, out_sem.at[n])
        for n, (src, dst) in enumerate(
            ((section_out, section_hbm), (igrad_ref, igrad_hbm), (cgrad_ref, cgrad_hbm))
        )
    ]
    leaving[0].start()
    leaving[1].start()

    def y_add(k, _):
        gy_copy(k, y).wait_recv()
        y_own[...] += y_in[k].astype(F32)
        return 0

    lax.fori_loop(1, Y, y_add, 0)
    z_out[...] = y_own[...]

    def gz_copy(j, dh, h_, sh, sz):
        where = (dp_at(x, h_, core), y * Z + HZ * core + j)
        return remote(z_out.at[j], z_in.at[sh, sz], gz_s.at[j, dh], gz_r.at[sh, sz], where)

    for dh in (*range(1, H), 0):
        h_ = lax.rem(zh + dh, H)
        for j in range(HZ):
            if dh:
                gz_copy(j, dh, h_, zh, z).start()
                continue
            mine = HZ * core + j == z

            @pl.when(mine)
            def _(j=j):
                z_in[zh, z] = z_out[j]

            @pl.when(jnp.logical_not(mine))
            def _(j=j, h_=h_):
                gz_copy(j, 0, h_, zh, z).start()

    def gf_copy(dx, core_, x_src, x_dst):
        return remote(quarters.at[x_src], quarters.at[x_src], gf_s.at[dx, core_], gf_r.at[x_src], (dp_at(x_dst, zh, core_), me))

    images = peers * dp_count(sizes)
    scale = 1.0 / float(images * pixels) ** 0.5

    @pl.when(active)
    def _():
        for h_ in range(H):
            for sz in range(Z):

                @pl.when(jnp.logical_not((zh == h_) & (z == sz)))
                def _(h_=h_, sz=sz):
                    gz_copy(0, 0, zh, h_, sz).wait_recv()

        total = z_in[0, 0]
        for h_ in range(H):
            for sz in range(Z):
                if h_ or sz:
                    total = total + z_in[h_, sz]
        quarters[x] = total * scale
        for dx in far_x:
            for other in range(2):
                gf_copy(dx, other, x, lax.rem(x + dx, X)).start()
        gf_copy(0, 1 - core, x, x).start()

    for x_ in range(X):

        @pl.when(jnp.logical_not(active & (x == x_)))
        def _(x_=x_):
            gf_copy(0, 0, x_, x).wait_recv()

    for x_ in range(X):
        first = (x_ % 2) * LANES
        cgrad_ref[x_ // 2, :, first : first + LANES] = quarters[x_]
    leaving[2].start()

    def a2a_left(k, _):
        a2a_copy(k, me, a2a_peer(k, 1)).wait_send()
        return 0

    lax.fori_loop(1, peers, a2a_left, 0)

    @pl.when(active)
    def _():
        for dz in range(1, Z):
            wz_copy(dz, around(z + dz, Z), me).wait_send()
        gf_copy(0, 1 - core, x, x).wait_send()
        for dx in range(1, X):
            for other in range(2):
                gf_copy(dx, other, x, lax.rem(x + dx, X)).wait_send()

    for j in range(HZ):
        for dh in range(1, H):
            gz_copy(j, dh, lax.rem(zh + dh, H), zh, z).wait_send()

        @pl.when(HZ * core + j != z)
        def _(j=j):
            gz_copy(j, 0, zh, zh, z).wait_send()

    def rest_left(k, _):
        y_ = lax.rem(y + k, Y)
        sy = around(y - k, Y)
        gc_copy(k, y_).wait_send()
        wc_copy(0, k, sy, x, core).wait_send()
        for dx in range(1, X):
            wc_copy(dx, k, sy, around(x - dx, X), core).wait_send()
            wx_copy(dx, k, sy, x, lax.rem(x + dx, X)).wait_send()
            gx_copy(dx, k, y_, lax.rem(x + dx, X)).wait_send()
        return 0

    lax.fori_loop(0, Y, rest_left, 0)

    def y_left(k, _):
        wy_copy(k, y, lax.rem(y + k, Y)).wait_send()
        gy_copy(k, lax.rem(y + k, Y)).wait_send()
        return 0

    lax.fori_loop(1, Y, y_left, 0)
    for copy in leaving:
        copy.wait()


def deliver(*refs):
    sources, targets, held, sems = refs[:3], refs[3:6], refs[6:9], refs[9]
    inward = [pltpu.make_async_copy(sources[n], held[n], sems.at[n]) for n in range(3)]
    outward = [pltpu.make_async_copy(held[n], targets[n], sems.at[n + 3]) for n in range(3)]
    for copy in inward:
        copy.start()
    for n in range(3):
        inward[n].wait()
        outward[n].start()
    for copy in outward:
        copy.wait()


def dp_count(sizes):
    return sizes[0] * sizes[1] * 2


def on_device(sizes, loader_rows, dest_list, row_counts, bucket_ids, conv_weight, out_grad):
    X, H, Y, Z = sizes
    HZ = Z // 2
    peers = Y * Z
    load, channels = loader_rows.shape[1:]
    pixels, out_width = out_grad.shape[1:]
    chunks = channels // LANES
    block = (load // peers + 1) * chunks
    rows_w = conv_weight.shape[0] // 2
    vmem = pltpu.VMEM
    sem = pltpu.SemaphoreType.DMA
    part = (HZ, rows_w, LANES)
    scratch = [
        vmem((load, channels), BF16),
        vmem((1, load), I32),
        vmem((1, 1), I32),
        vmem((1, 1), I32),
        vmem((pixels, out_width), BF16),
        vmem((pixels, out_width), F32),
        vmem((pixels, out_width), BF16),
        vmem((pixels, channels), BF16),
        vmem((2, rows_w, out_width), F32),
        vmem((peers * block, LANES), F32),
        vmem((peers, block, LANES), BF16),
        vmem((peers, block, LANES), BF16),
        vmem((X, peers, rows_w, LANES), BF16),
        vmem((TAPS, pixels, pixels), BF16),
        vmem((TAPS, pixels, out_width), BF16),
        vmem((pixels, channels), F32),
        vmem((8, channels), F32),
        vmem((pixels, channels), BF16),
        vmem((channels, pixels), BF16),
        vmem((pixels, channels), F32),
        vmem((TAPS * channels, out_width), F32),
        vmem((Y, HZ, 2, rows_w, out_width), BF16),
        vmem((Y, HZ, 2, rows_w, out_width), BF16),
        vmem((X, Y, *part), BF16),
        vmem((Y, *part), F32),
        vmem((X, Y, *part), BF16),
        vmem((Y, *part), BF16),
        vmem(part, F32),
        vmem((Y, *part), BF16),
        vmem(part, F32),
        vmem((H, Z, rows_w, LANES), F32),
        vmem((X, rows_w, LANES), F32),
        sem((5,)), sem((3,)), sem,
        sem((peers,)), sem((peers,)),
        sem((Z,)), sem((Z,)),
        sem((Y,)), sem((Y,)),
        sem((X, Y)), sem((X, Y)),
        sem((X, Y)), sem((X, Y)),
        sem((Y,)), sem((Y,)),
        sem((X, Y)), sem((X, Y)),
        sem((Y,)), sem((Y,)),
        sem((HZ, H)), sem((H, Z)),
        sem((X, 2)), sem((X,)),
    ]
    anywhere = pl.BlockSpec(memory_space=pl.ANY)
    flops = 2 * pixels * out_width * channels * TAPS * 3
    section, igrad, cgrad = pl.pallas_call(
        functools.partial(kernel, sizes),
        out_shape=(
            jax.ShapeDtypeStruct((pixels, out_width), BF16),
            jax.ShapeDtypeStruct((pixels, channels), BF16),
            jax.ShapeDtypeStruct((2, rows_w, out_width), F32),
        ),
        in_specs=[anywhere] * 6,
        out_specs=(anywhere,) * 3,
        scratch_shapes=scratch,
        compiler_params=pltpu.CompilerParams(
            collective_id=0, has_side_effects=True, vmem_limit_bytes=60 * 2**20
        ),
        cost_estimate=pl.CostEstimate(flops=flops, bytes_accessed=2**21, transcendentals=0),
        name="residual_section",
    )(
        loader_rows[0],
        dest_list,
        row_counts,
        bucket_ids,
        conv_weight.reshape(2, rows_w, out_width),
        out_grad[0],
    )
    section, igrad, cgrad = pl.pallas_call(
        deliver,
        out_shape=tuple(jax.ShapeDtypeStruct(a.shape, a.dtype) for a in (section, igrad, cgrad)),
        in_specs=[anywhere] * 3,
        out_specs=(anywhere,) * 3,
        scratch_shapes=[*(vmem(a.shape, a.dtype) for a in (section, igrad, cgrad)), sem((6,))],
        name="deliver",
    )(section, igrad, cgrad)
    return section[None], igrad[None], cgrad.reshape(conv_weight.shape)


def solution(mesh):
    sizes = layout(mesh)
    in_specs = (
        P("dp", "fsdp", None),
        P("dp", "fsdp"),
        P("dp", "fsdp"),
        P("dp", "fsdp"),
        P("fsdp", None),
        P("dp", "fsdp", None),
    )
    out_specs = (P("dp", "fsdp", None), P("dp", "fsdp", None), P("fsdp", None))
    return jax.shard_map(
        functools.partial(on_device, sizes), mesh=mesh, in_specs=in_specs, out_specs=out_specs, check_vma=False
    )
```
